32 devices in a mesh: seq: 8 (over z, y), head: 4 (over x, core).
Axes of the slice: x: 2, y: 2, z: 4, core: 2. Of those that a mesh axis runs over, the one named last changes fastest.
Arguments:
- queries: bfloat16 [1280, 3072], P('seq', 'head'), may hold values from -240 to 240
- latent_rope: bfloat16 [1280, 576], P('seq'), may hold values from -4 to 4
- w_uk: bfloat16 [512, 2048], P(None, 'head'), may hold values from -0.25 to 0.25
- w_uv: bfloat16 [512, 2048], P(None, 'head'), may hold values from -0.25 to 0.25
- d_out: bfloat16 [1280, 2048], P('seq', 'head'), may hold values from -6 to 6
- block_order: int32 [16], replicated, may hold values from 0 to 15, as said below
- block_doc: int32 [16], replicated, may hold values from 0 to 2, never falling along the last dimension, each value on 1 to 8 neighbouring positions
Outputs:
- d_queries: bfloat16 [1280, 3072], P('seq', 'head')
- d_latent: float32 [1280, 576], P('seq')
- d_w_uk: float32 [512, 2048], P(None, 'head')
- d_w_uv: float32 [512, 2048], P(None, 'head')
The draws below stay inside these ranges and needn't reach their ends.
Inputs may be any that keep to these rules, and one draw needn't show every extreme that they name: block_order holds every sequence block once, and block_order[2 s] + block_order[2 s + 1] = 15 for every s. `block_doc`: never falls along the sequence blocks.
All inputs are finite; a program needn't handle non-finite values.
Results may differ from the reference program's by a relative error of at most 0.017.
Values may be sent and summed in bfloat16 or wider, within the bound.
No kernel may reach another device: no remote copies, remote signals or barrier semaphores. Data moves between devices by JAX's collectives and lax.ppermute only.
A program may use at most 128 MiB of HBM per device.

```python
import math
import jax
import jax.numpy as jnp
import numpy as np
from jax import lax

D_LAT = 512
ROPE = 64
NOPE = 128
VDIM = 128
HEADS = 16
TOK_DEV = 160
HALF = 80
TOKENS = 1280
BLOCKS = 16
N_SEQ = 8


def draw_latent_rope(key, part):
    key = jax.random.fold_in(key, 7)
    first_key, second_key = jax.random.split(key)
    latent = jnp.clip(jax.random.normal(first_key, (TOKENS, D_LAT), jnp.float32), -4.0, 4.0)
    rotary = jnp.clip(jax.random.normal(second_key, (TOKENS, ROPE), jnp.float32), -4.0, 4.0)
    return jnp.concatenate([latent, rotary], axis=1).astype(jnp.bfloat16)


def draw_queries(key, part):
    key = jax.random.fold_in(key, 13)
    first_key = jax.random.fold_in(key, 0)
    drawn = jnp.clip(jax.random.normal(first_key, (TOKENS // 2, 2, HEADS, NOPE + ROPE), jnp.float32), -4.0, 4.0)
    return drawn.reshape(TOKENS, HEADS * (NOPE + ROPE)).astype(jnp.bfloat16)


def draw_block_order(key, part):
    key = jax.random.fold_in(key, 29)
    pairs = jax.random.permutation(key, BLOCKS // 2)
    ordered = jnp.stack([pairs, BLOCKS - 1 - pairs], axis=1).reshape(BLOCKS)
    return ordered.astype(jnp.int32)


def steps_of(key, dims, cuts, smallest, top_value):
    loudness = 1.0
    for axis_at, parts in cuts:
        draws = jax.random.uniform(jax.random.fold_in(jax.random.fold_in(key, 6), axis_at), (parts,), jnp.float32, smallest / len(cuts), top_value / len(cuts))
        loudness = loudness * jnp.repeat(jnp.exp(draws), dims[axis_at] // parts).reshape((-1,) + (1,) * (len(dims) - 1 - axis_at))
    return loudness


def length_profile(number_of, total, most, lean):
    weights = [(1 << 20) // math.isqrt(grade ** lean) + 1 for grade in range(2, number_of + 1)]
    spare, counts = total - most - (number_of - 1), [1] * (number_of - 1)
    while spare > 0:
        movable = [i for i in range(number_of - 1) if counts[i] < most]
        pool, budget = sum([weights[i] for i in movable]), spare
        for i in movable:
            addition = min(most - counts[i], max(1, budget * weights[i] // pool), spare)
            counts[i] = counts[i] + addition
            spare = spare - addition
    return np.array([most] + counts)


def uneven(rng, amount, total, bound, lean):
    if amount == 2:
        one = jax.random.randint(rng, (), max(1, total - bound), min(bound, total - 1) + 1)
        return jnp.stack([one, total - one])
    lengths = jnp.asarray(length_profile(amount, total, bound, lean), jnp.int32)
    twos = (amount - 1) // 2
    donor, taker = lengths[1:1 + 2 * twos:2], lengths[2:2 + 2 * twos:2]
    room = jnp.minimum(donor - 1, bound - taker)
    moved = jax.random.randint(jax.random.fold_in(rng, 1), (twos,), 0, 1 << 20) % (room + 1)
    lengths = lengths.at[1:1 + 2 * twos:2].set(donor - moved).at[2:2 + 2 * twos:2].set(taker + moved)
    return lengths[jax.random.permutation(jax.random.fold_in(rng, 2), amount)]


def centred(own_key, shape, width, reach, pieces=(), kind=jnp.bfloat16):
    array = width * jax.random.normal(own_key, shape, jnp.float32)
    if pieces:
        array = array * steps_of(own_key, shape, pieces, -0.22, 0.18)
    return jnp.clip(array, -reach, reach).astype(kind)


def setup_inputs(seed: int = 0) -> dict:
    key_of = jax.random.split(jax.random.key(seed), 8)
    return {
        "queries": draw_queries(jax.random.fold_in(key_of[7], 71), 0),
        "latent_rope": draw_latent_rope(jax.random.fold_in(key_of[7], 71), 0),
        "w_uk": centred(key_of[2], (D_LAT, HEADS * NOPE), D_LAT ** -0.5, 0.25, ((1, 4),)),
        "w_uv": centred(key_of[3], (D_LAT, HEADS * VDIM), D_LAT ** -0.5, 0.25, ((1, 4),)),
        "d_out": centred(key_of[4], (TOKENS, HEADS * VDIM), 1.0, 6.0, ((0, 8), (1, 4))),
        "block_order": draw_block_order(jax.random.fold_in(key_of[7], 71), 0),
        "block_doc": jnp.searchsorted(jnp.cumsum(uneven(key_of[6], 3, BLOCKS, BLOCKS // 2, 0)), jnp.arange(BLOCKS), side="right").astype(jnp.int32),
    }


NEG_FILL = -1e30


def keep_low(values_in):
    lowered = lax.optimization_barrier(values_in.astype(jnp.bfloat16))
    return lowered.astype(jnp.float32)


def reference(queries, latent_rope, w_uk, w_uv, d_out, block_order, block_doc):
    row_index = jnp.arange(TOKENS, dtype=jnp.int32)
    seq_block = block_order[row_index // HALF]
    position = seq_block * HALF + row_index % HALF
    document = block_doc[seq_block]
    latent = latent_rope[:, :D_LAT]
    key_rope = latent_rope[:, D_LAT:].astype(jnp.float32)
    key_nope = jnp.dot(latent, w_uk, preferred_element_type=jnp.float32).astype(jnp.bfloat16)
    values_up = jnp.dot(latent, w_uv, preferred_element_type=jnp.float32).astype(jnp.bfloat16)
    key_nope = key_nope.astype(jnp.float32).reshape(TOKENS, HEADS, NOPE)
    values_up = values_up.astype(jnp.float32).reshape(TOKENS, HEADS, VDIM)
    score_scale = (NOPE + ROPE) ** -0.5
    query_groups = queries.reshape(N_SEQ, TOK_DEV, HEADS, NOPE + ROPE)
    grad_groups = d_out.reshape(N_SEQ, TOK_DEV, HEADS, VDIM)
    pos_groups = position.reshape(N_SEQ, TOK_DEV)
    doc_groups = document.reshape(N_SEQ, TOK_DEV)

    def group_step(carry, inputs):
        nope_sum, value_sum, rope_sum = carry
        query_rows, grad_rows, query_pos, query_doc = inputs
        query_full = query_rows.astype(jnp.float32)
        grad_full = grad_rows.astype(jnp.float32)
        scores = jnp.einsum('qhd,khd->hqk', query_full[:, :, :NOPE], key_nope)
        scores = (scores + jnp.einsum('qhd,kd->hqk', query_full[:, :, NOPE:], key_rope)) * score_scale
        visible = (query_pos[:, None] >= position[None, :]) & (query_doc[:, None] == document[None, :])
        scores = jnp.where(visible[None], scores, NEG_FILL)
        row_max = jnp.max(scores, axis=2, keepdims=True)
        expo = jnp.where(visible[None], jnp.exp(scores - row_max), 0.0)
        probs = expo / jnp.sum(expo, axis=2, keepdims=True)
        probs_low = keep_low(probs)
        attended = jnp.einsum('hqk,khd->hqd', probs_low, values_up)
        delta = jnp.einsum('qhd,hqd->hq', grad_full, attended)
        grad_probs = jnp.einsum('qhd,khd->hqk', grad_full, values_up)
        grad_scores = keep_low(probs * (grad_probs - delta[:, :, None]) * score_scale)
        grad_nope = jnp.einsum('hqk,khd->qhd', grad_scores, key_nope)
        grad_rope = jnp.einsum('hqk,kd->qhd', grad_scores, key_rope)
        grad_query = jnp.concatenate([grad_nope, grad_rope], axis=2).astype(jnp.bfloat16)
        key_grad = jnp.einsum('hqk,qhd->khd', grad_scores, query_full)
        knope = keep_low(key_grad[:, :, :NOPE]).reshape(TOKENS, HEADS * NOPE)
        rope_part = jnp.sum(key_grad[:, :, NOPE:], axis=1)
        vgrad = keep_low(jnp.einsum('hqk,qhd->khd', probs_low, grad_full)).reshape(TOKENS, HEADS * VDIM)
        return (nope_sum + knope, value_sum + vgrad, rope_sum + rope_part), grad_query

    start_carry = (jnp.zeros((TOKENS, HEADS * NOPE), jnp.float32),
                   jnp.zeros((TOKENS, HEADS * VDIM), jnp.float32),
                   jnp.zeros((TOKENS, ROPE), jnp.float32))
    (nope_sum, value_sum, rope_sum), grad_queries = lax.scan(
        group_step, start_carry, (query_groups, grad_groups, pos_groups, doc_groups))
    d_queries = grad_queries.reshape(TOKENS, HEADS * (NOPE + ROPE))
    highest = lax.Precision.HIGHEST
    uk_full = w_uk.astype(jnp.float32)
    uv_full = w_uv.astype(jnp.float32)
    latent_full = latent.astype(jnp.float32)
    main_part = jnp.dot(nope_sum, uk_full.T, precision=highest) + jnp.dot(value_sum, uv_full.T, precision=highest)
    d_latent = jnp.concatenate([main_part, rope_sum], axis=1)
    d_w_uk = jnp.dot(latent_full.T, nope_sum, precision=highest)
    d_w_uv = jnp.dot(latent_full.T, value_sum, precision=highest)
    return (d_queries, d_latent, d_w_uk, d_w_uv)
```

```python
import functools
import math

import jax
import jax.numpy as jnp
from jax import lax
from jax.experimental import pallas as pl
from jax.experimental.pallas import tpu as pltpu
from jax.sharding import PartitionSpec as P

D_LAT = 512
ROPE = 64
NOPE = 128
VDIM = 128
WIDTH = NOPE + ROPE
SCALE = WIDTH ** (-0.5)
SCALE_LOG2 = SCALE * math.log2(math.e)
NEG_FILL = -1e30
TILE = 256
VMEM_BYTES = 60 * 1024 * 1024
BY_COLUMNS = (((1,), (1,)), ((), ()))
BY_ROWS = (((1,), (0,)), ((), ()))
SMEM = pl.BlockSpec(memory_space=pltpu.SMEM)
VMEM = pl.BlockSpec(memory_space=pltpu.VMEM)
HBM = pl.BlockSpec(memory_space=pl.ANY)


def dot(a, b, dims):
    return lax.dot_general(a, b, dims, preferred_element_type=jnp.float32)


def head_queries(x_ref, rows, head, nope_at, rope_at):
    nope = x_ref[rows, nope_at + head * NOPE : nope_at + (head + 1) * NOPE]
    rope = x_ref[rows, rope_at + head * ROPE : rope_at + (head + 1) * ROPE]
    return jnp.concatenate([nope, rope], axis=1)


def project_kernel(
    masks, half, heads, order_ref, low_ref, where_ref, mine_ref, other_ref, wk_ref, wv_ref, x_ref,
    keys_ref, values_ref, turned_ref, dq_ref, latent, sem,
):
    blocks = 2 * len(masks)
    total = blocks * half
    me, core = where_ref[0], where_ref[1]
    copies = []
    for number, mask in enumerate(masks):
        for side, source in enumerate((mine_ref, other_ref)):
            block = order_ref[2 * (me ^ mask) + (core ^ side)]
            target = latent.at[pl.ds(pl.multiple_of(block * half, 16), half), :]
            copy = pltpu.make_async_copy(
                source.at[pl.ds(number * half, half), :], target, sem.at[2 * number + side]
            )
            copy.start()
            copies.append(copy)
    for copy in copies:
        copy.wait()
    for first in range(0, total, TILE):
        rows = pl.ds(first, TILE)
        part = latent[rows, :D_LAT]
        rope = latent[rows, D_LAT:]
        up_keys = dot(part, wk_ref[...], BY_ROWS).astype(jnp.bfloat16)
        for head in range(heads):
            keys_ref[head, rows, :] = jnp.concatenate(
                [up_keys[:, head * NOPE : (head + 1) * NOPE], rope], axis=1
            )
        values_ref[rows, :] = dot(part, wv_ref[...], BY_ROWS).astype(jnp.bfloat16)
        turned_ref[:, first : first + TILE] = part.T
    span = (blocks // 2) * half
    rope_at = heads * NOPE
    grad_at = heads * WIDTH
    for side in range(2):
        block = order_ref[2 * me + side]
        start = pl.multiple_of(jnp.maximum(block - (blocks // 2 - 1), 0) * half, 16)
        window = pl.ds(start, span)
        key_pos = start + lax.broadcasted_iota(jnp.int32, (half, span), 1)
        query_pos = block * half + lax.broadcasted_iota(jnp.int32, (half, span), 0)
        seen = (key_pos <= query_pos) & (key_pos >= low_ref[block] * half)
        bias = jnp.where(seen, 0.0, NEG_FILL)
        rows = pl.ds(side * half, half)
        outs = []
        for head in range(heads):
            query = head_queries(x_ref, rows, head, 0, rope_at)
            grad = x_ref[rows, grad_at + head * VDIM : grad_at + (head + 1) * VDIM]
            keys = keys_ref[head, window, :]
            values = values_ref[window, head * VDIM : (head + 1) * VDIM]
            scores = dot(query, keys, BY_COLUMNS) * SCALE_LOG2 + bias
            expo = jnp.exp2(scores - jnp.max(scores, axis=1, keepdims=True))
            probs = expo * (1.0 / jnp.sum(expo, axis=1, keepdims=True))
            grad_probs = dot(grad, values, BY_COLUMNS)
            delta = jnp.sum(probs * grad_probs, axis=1, keepdims=True)
            grad_scores = (probs * (grad_probs - delta) * SCALE).astype(jnp.bfloat16)
            outs.append(dot(grad_scores, keys, BY_ROWS).astype(jnp.bfloat16))
        dq_ref[rows, :] = jnp.concatenate(outs, axis=1)


def key_kernel(masks, half, heads, first_head, here, order_ref, where_ref, *refs):
    count = len(masks)
    x_refs = refs[:count]
    low_ref, keys_ref, values_ref, wk_ref, wv_ref = refs[count : count + 5]
    dk_ref, dv_ref, dlat_ref = refs[count + 5 : count + 8]
    x_all, sum_nope, sum_value, sum_rope, sem = refs[count + 8 :]
    blocks = 2 * count
    total = blocks * half
    me = where_ref[0]
    rope_at = here * NOPE
    grad_at = rope_at + heads * ROPE
    if here == heads:
        columns = ((0, 0, heads * (WIDTH + VDIM)),)
    else:
        columns = (
            (first_head * NOPE, 0, here * NOPE),
            (heads * NOPE, rope_at, heads * ROPE),
            (heads * WIDTH + first_head * VDIM, grad_at, here * VDIM),
        )
    copies = []
    for number, mask in enumerate(masks):
        for side in range(2):
            block = order_ref[2 * (me ^ mask) + side]
            rows = pl.ds(pl.multiple_of(block * half, 16), half)
            for piece, (source, target, wide) in enumerate(columns):
                copy = pltpu.make_async_copy(
                    x_refs[number].at[pl.ds(side * half, half), pl.ds(source, wide)],
                    x_all.at[rows, pl.ds(target, wide)],
                    sem.at[(2 * number + side) * len(columns) + piece],
                )
                copy.start()
                copies.append(copy)
    sum_nope[...] = jnp.zeros_like(sum_nope)
    sum_value[...] = jnp.zeros_like(sum_value)
    sum_rope[...] = jnp.zeros_like(sum_rope)
    for copy in copies:
        copy.wait()

    def tile(first, start, span):
        window = pl.ds(start, span)
        rows = pl.ds(first, TILE)
        key_pos = start + lax.broadcasted_iota(jnp.int32, (span, TILE), 0)
        query_pos = first + lax.broadcasted_iota(jnp.int32, (span, TILE), 1)
        seen = (key_pos <= query_pos) & (key_pos >= low_ref[:, rows])
        bias = jnp.where(seen, 0.0, NEG_FILL)
        for head in range(here):
            lanes = slice(head * NOPE, (head + 1) * NOPE)
            query = jnp.concatenate(
                [
                    x_all[rows, lanes],
                    x_all[rows, rope_at + (first_head + head) * ROPE : rope_at + (first_head + head + 1) * ROPE],
                ],
                axis=1,
            )
            grad = x_all[rows, grad_at + head * VDIM : grad_at + (head + 1) * VDIM]
            keys = keys_ref[head, window, :]
            values = values_ref[window, lanes]
            scores = dot(keys, query, BY_COLUMNS) * SCALE_LOG2 + bias
            expo = jnp.exp2(scores - jnp.max(scores, axis=0, keepdims=True))
            probs = expo * (1.0 / jnp.sum(expo, axis=0, keepdims=True))
            grad_probs = dot(values, grad, BY_COLUMNS)
            delta = jnp.sum(probs * grad_probs, axis=0, keepdims=True)
            grad_scores = (probs * (grad_probs - delta) * SCALE).astype(jnp.bfloat16)
            sum_value[window, lanes] += dot(probs.astype(jnp.bfloat16), grad, BY_ROWS)
            key_grad = dot(grad_scores, query, BY_ROWS)
            sum_nope[window, lanes] += key_grad[:, :NOPE]
            sum_rope[window, :] += key_grad[:, NOPE:]

    reach = (blocks // 2 - 1) * half
    if total <= 8 * TILE:
        for first in range(0, total, TILE):
            start = max(first // half * half - reach, 0)
            tile(first, start, first + TILE - start)
    else:
        span = -(-(reach + half + TILE) // 16) * 16

        def step(number, carry):
            first = pl.multiple_of(number * TILE, TILE)
            start = jnp.clip(first + TILE - span, 0, total - span)
            tile(first, pl.multiple_of(start, 16), span)
            return carry

        lax.fori_loop(0, total // TILE, step, 0)
    dk_ref[...] = sum_nope[...].astype(jnp.bfloat16)
    dv_ref[...] = sum_value[...].astype(jnp.bfloat16)
    for side in range(2):
        block = order_ref[2 * me + side]
        rows = pl.ds(pl.multiple_of(block * half, 16), half)
        out = dot(dk_ref[rows, :], wk_ref[...], BY_COLUMNS)
        out = out + dot(dv_ref[rows, :], wv_ref[...], BY_COLUMNS)
        dlat_ref[pl.ds(side * half, half), :] = jnp.concatenate([out, sum_rope[rows, :]], axis=1)


def swap(array, axis, mask):
    size = lax.axis_size(axis)
    return lax.ppermute(array, axis, [(i, i ^ mask) for i in range(size)])


def shards(queries, latent_rope, w_uk, w_uv, d_out, block_order, block_doc):
    local_rows = queries.shape[0]
    heads = w_uk.shape[1] // NOPE
    devices = lax.axis_size("seq")
    half = local_rows // 2
    total = local_rows * devices
    me = lax.axis_index("seq")
    core = lax.axis_index("head") % 2
    where = jnp.stack([me, core]).astype(jnp.int32)
    low = jnp.sum((block_doc[None, :] < block_doc[:, None]).astype(jnp.int32), axis=1)
    low_rows = jnp.repeat(low * half, half).reshape(1, total)

    latent_masks = [0]
    mine = lax.dynamic_slice_in_dim(latent_rope, core * half, half, axis=0)
    step = devices // 2
    while step:
        mine = jnp.concatenate([mine, swap(mine, "seq", step)], axis=0)
        latent_masks = latent_masks + [m ^ step for m in latent_masks]
        step //= 2
    other = swap(mine, "head", 1)

    by_head = queries.reshape(local_rows, heads, WIDTH)
    packed = jnp.concatenate(
        [
            by_head[:, :, :NOPE].reshape(local_rows, heads * NOPE),
            by_head[:, :, NOPE:].reshape(local_rows, heads * ROPE),
            d_out,
        ],
        axis=1,
    )
    far = [packed] + [swap(packed, "seq", m) for m in range(2, devices, 2)]
    near = [swap(x, "seq", 1) for x in far]
    pieces = far + near
    masks = list(range(0, devices, 2)) + list(range(1, devices, 2))

    bf16 = jnp.bfloat16
    params = pltpu.CompilerParams(vmem_limit_bytes=VMEM_BYTES)
    keys, values, turned, d_queries = pl.pallas_call(
        functools.partial(project_kernel, latent_masks, half, heads),
        out_shape=(
            jax.ShapeDtypeStruct((heads, total, WIDTH), bf16),
            jax.ShapeDtypeStruct((total, heads * VDIM), bf16),
            jax.ShapeDtypeStruct((D_LAT, total), bf16),
            jax.ShapeDtypeStruct((local_rows, heads * WIDTH), bf16),
        ),
        in_specs=[SMEM, SMEM, SMEM, HBM, HBM, VMEM, VMEM, VMEM],
        out_specs=(VMEM, VMEM, VMEM, VMEM),
        scratch_shapes=[
            pltpu.VMEM((total, D_LAT + ROPE), bf16),
            pltpu.SemaphoreType.DMA((2 * devices,)),
        ],
        compiler_params=params,
        name="project",
    )(block_order, low, where, mine, other, w_uk, w_uv, packed)

    here = heads if total <= 8 * TILE else 1
    parts = 1 if here == heads else 3
    dks, dvs, dlat = [], [], 0.0
    for first_head in range(0, heads, here):
        lanes = slice(first_head * NOPE, (first_head + here) * NOPE)
        dk, dv, share = pl.pallas_call(
            functools.partial(key_kernel, masks, half, heads, first_head, here),
            out_shape=(
                jax.ShapeDtypeStruct((total, here * NOPE), bf16),
                jax.ShapeDtypeStruct((total, here * VDIM), bf16),
                jax.ShapeDtypeStruct((local_rows, D_LAT + ROPE), jnp.float32),
            ),
            in_specs=[SMEM, SMEM] + [HBM] * devices + [VMEM] * 5,
            out_specs=(VMEM, VMEM, VMEM),
            scratch_shapes=[
                pltpu.VMEM((total, here * (NOPE + VDIM) + heads * ROPE), bf16),
                pltpu.VMEM((total, here * NOPE), jnp.float32),
                pltpu.VMEM((total, here * VDIM), jnp.float32),
                pltpu.VMEM((total, ROPE), jnp.float32),
                pltpu.SemaphoreType.DMA((2 * devices * parts,)),
            ],
            compiler_params=params,
            name="keys",
        )(
            block_order, where, *pieces, low_rows,
            keys[first_head : first_head + here], values[:, lanes], w_uk[:, lanes], w_uv[:, lanes],
        )
        dks.append(dk)
        dvs.append(dv)
        dlat = dlat + share
    dk = jnp.concatenate(dks, axis=1)
    dv = jnp.concatenate(dvs, axis=1)
    step = 1
    while step < lax.axis_size("head"):
        sent = dlat.astype(bf16)
        dlat = sent.astype(jnp.float32) + swap(sent, "head", step).astype(jnp.float32)
        step *= 2
    return (d_queries, dlat, dot(turned, dk, BY_ROWS), dot(turned, dv, BY_ROWS))


def solution(mesh):
    return jax.shard_map(
        shards,
        mesh=mesh,
        in_specs=(
            P("seq", "head"),
            P("seq", None),
            P(None, "head"),
            P(None, "head"),
            P("seq", "head"),
            P(),
            P(),
        ),
        out_specs=(P("seq", "head"), P("seq", None), P(None, "head"), P(None, "head")),
        check_vma=False,
    )
```

```python
import functools
import math

import jax
import jax.numpy as jnp
from jax import lax
from jax.experimental import pallas as pl
from jax.experimental.pallas import tpu as pltpu
from jax.sharding import PartitionSpec as P

D_LAT = 512
ROPE = 64
NOPE = 128
VDIM = 128
WIDTH = NOPE + ROPE
SCALE = WIDTH ** (-0.5)
SCALE_LOG2 = SCALE * math.log2(math.e)
NEG_FILL = -1e30
TILE = 256
GRAIN = 128
LAT_LANES = 640
BY_COLUMNS = (((1,), (1,)), ((), ()))
BY_ROWS = (((1,), (0,)), ((), ()))
SMEM = pl.BlockSpec(memory_space=pltpu.SMEM)
VMEM = pl.BlockSpec(memory_space=pltpu.VMEM)
HBM = pl.BlockSpec(memory_space=pl.ANY)


def dot(a, b, dims):
    return lax.dot_general(a, b, dims, preferred_element_type=jnp.float32)


def project_kernel(
    devices, half, heads, pair, order_ref, low_ref, where_ref, mine_ref, other_ref, wk_in, wv_in, *refs
):
    x_refs = refs[: heads // pair]
    keys_ref, values_ref, turned_ref, dq_ref, latent, wk_ref, wv_ref, sem, weight_sem = refs[heads // pair :]
    blocks = 2 * devices
    total = blocks * half
    me, core = where_ref[0], where_ref[1]
    copies = [
        pltpu.make_async_copy(wk_in, wk_ref, weight_sem.at[0]),
        pltpu.make_async_copy(wv_in, wv_ref, weight_sem.at[1]),
    ]
    for copy in copies:
        copy.start()
    masks = [0]
    for bit in reversed(range(devices.bit_length() - 1)):
        masks = masks + [m ^ (1 << bit) for m in masks]
    for number, mask in enumerate(masks):
        for side, source in enumerate((mine_ref, other_ref)):
            block = order_ref[2 * (me ^ mask) + (core ^ side)]
            copy = pltpu.make_async_copy(
                source.at[pl.ds(number * half, half), :],
                latent.at[pl.ds(pl.multiple_of(block * half, 16), half), :],
                sem.at[2 * number + side],
            )
            copy.start()
            copies.append(copy)
    for copy in copies:
        copy.wait()
    for first in range(0, total, TILE):
        rows = pl.ds(first, TILE)
        part = latent[rows, :D_LAT]
        rope = latent[rows, D_LAT : D_LAT + ROPE]
        up_keys = dot(part, wk_ref[...], BY_ROWS).astype(jnp.bfloat16)
        for head in range(heads):
            keys_ref[head, rows, :] = jnp.concatenate(
                [up_keys[:, head * NOPE : (head + 1) * NOPE], rope], axis=1
            )
        values_ref[rows, :] = dot(part, wv_ref[...], BY_ROWS).astype(jnp.bfloat16)
        turned_ref[:, first : first + TILE] = part.T
    span = (blocks // 2) * half
    grad_at = pair * WIDTH
    for side in range(2):
        block = order_ref[2 * me + side]
        start = pl.multiple_of(jnp.maximum(block - (blocks // 2 - 1), 0) * half, 16)
        window = pl.ds(start, span)
        key_pos = start + lax.broadcasted_iota(jnp.int32, (half, span), 1)
        query_pos = block * half + lax.broadcasted_iota(jnp.int32, (half, span), 0)
        seen = (key_pos <= query_pos) & (key_pos >= low_ref[block] * half)
        bias = jnp.where(seen, 0.0, NEG_FILL)
        rows = pl.ds(side * half, half)
        outs = []
        for head in range(heads):
            x_ref, at = x_refs[head // pair], head % pair
            query = x_ref[rows, at * WIDTH : (at + 1) * WIDTH]
            grad = x_ref[rows, grad_at + at * VDIM : grad_at + (at + 1) * VDIM]
            keys = keys_ref[head, window, :]
            values = values_ref[window, head * VDIM : (head + 1) * VDIM]
            scores = dot(query, keys, BY_COLUMNS) * SCALE_LOG2 + bias
            expo = jnp.exp2(scores - jnp.max(scores, axis=1, keepdims=True))
            probs = expo * (1.0 / jnp.sum(expo, axis=1, keepdims=True))
            grad_probs = dot(grad, values, BY_COLUMNS)
            delta = jnp.sum(probs * grad_probs, axis=1, keepdims=True)
            grad_scores = (probs * (grad_probs - delta) * SCALE).astype(jnp.bfloat16)
            outs.append(dot(grad_scores, keys, BY_ROWS).astype(jnp.bfloat16))
        dq_ref[rows, :] = jnp.concatenate(outs, axis=1)


def key_kernel(devices, half, here, begun, low_ref, order_ref, source_ref, *refs):
    x_refs = refs[:devices]
    low_rows_ref, *sources = refs[devices : devices + 5]
    dk_ref, dv_ref, dlat_ref = refs[devices + 5 + begun : devices + 8 + begun]
    x_all, sum_nope, sum_value, sum_rope, sem = refs[devices + 8 + begun : devices + 13 + begun]
    *held, held_sem = refs[devices + 13 + begun :]
    keys_ref, values_ref, wk_ref, wv_ref = held
    loads = [
        pltpu.make_async_copy(source, target, held_sem.at[number])
        for number, (source, target) in enumerate(zip(sources, held))
    ]
    for copy in loads:
        copy.start()
    blocks = 2 * devices
    total = blocks * half
    grad_at = here * WIDTH
    copies = []
    for number in range(devices):
        for side in range(2):
            block = order_ref[2 * source_ref[number] + side]
            rows = pl.ds(pl.multiple_of(block * half, 16), half)
            copy = pltpu.make_async_copy(
                x_refs[number].at[pl.ds(side * half, half), :],
                x_all.at[rows, :],
                sem.at[2 * number + side],
            )
            copy.start()
            copies.append(copy)
    sum_nope[...] = jnp.zeros_like(sum_nope)
    sum_value[...] = jnp.zeros_like(sum_value)
    sum_rope[...] = jnp.zeros_like(sum_rope)
    for copy in loads[:2] + copies:
        copy.wait()

    def tile(first, start, span):
        window = pl.ds(start, span)
        rows = pl.ds(first, TILE)
        key_pos = start + lax.broadcasted_iota(jnp.int32, (span, TILE), 0)
        query_pos = first + lax.broadcasted_iota(jnp.int32, (span, TILE), 1)
        seen = (key_pos <= query_pos) & (key_pos >= low_rows_ref[:, rows])
        bias = jnp.where(seen, 0.0, NEG_FILL)
        def begin(head):
            lanes = slice(head * NOPE, (head + 1) * NOPE)
            query = x_all[rows, head * WIDTH : (head + 1) * WIDTH]
            grad = x_all[rows, grad_at + head * VDIM : grad_at + (head + 1) * VDIM]
            scores = dot(keys_ref[head, window, :], query, BY_COLUMNS)
            return lanes, query, grad, scores, dot(values_ref[window, lanes], grad, BY_COLUMNS)

        def middle(lanes, query, grad, scores, grad_probs):
            scores = scores * SCALE_LOG2 + bias
            expo = jnp.exp2(scores - jnp.max(scores, axis=0, keepdims=True))
            inverse = 1.0 / jnp.sum(expo, axis=0, keepdims=True)
            delta = jnp.sum(expo * grad_probs, axis=0, keepdims=True) * inverse
            probs = expo * inverse
            grad_scores = (probs * (grad_probs - delta)).astype(jnp.bfloat16)
            return lanes, query, grad, probs.astype(jnp.bfloat16), grad_scores

        def end(lanes, query, grad, probs, grad_scores):
            sum_value[window, lanes] += dot(probs, grad, BY_ROWS)
            key_grad = dot(grad_scores, query, BY_ROWS)
            sum_nope[window, lanes] += key_grad[:, :NOPE]
            return key_grad[:, NOPE:]

        rope = 0.0
        begun_heads = [begin(0)]
        for head in range(here):
            if head + 1 < here:
                begun_heads.append(begin(head + 1))
            rope = rope + end(*middle(*begun_heads[head]))
        sum_rope[window, :] += rope

    def step(number, carry):
        first = pl.multiple_of(number * TILE, TILE)
        oldest = low_ref[first // half] * half
        need = (first + TILE - oldest + GRAIN - 1) // GRAIN
        for size in sizes:
            below = sizes[sizes.index(size) - 1] if size != sizes[0] else 0

            @pl.when((need <= size) & (need > below))
            def _(size=size):
                start = jnp.maximum(first + TILE - size * GRAIN, 0)
                tile(first, pl.multiple_of(start, 16), size * GRAIN)

        return carry

    most = -(-(devices * half + TILE) // GRAIN)
    sizes = list(range(TILE // GRAIN, most + 1, max(1, most // 8)))
    if sizes[-1] != most:
        sizes.append(most)
    lax.fori_loop(0, total // TILE, step, 0)
    dk_ref[...] = (sum_nope[...] * SCALE).astype(jnp.bfloat16)
    dv_ref[...] = sum_value[...].astype(jnp.bfloat16)
    for copy in loads[2:]:
        copy.wait()
    for side in range(2):
        block = order_ref[2 * source_ref[0] + side]
        rows = pl.ds(pl.multiple_of(block * half, 16), half)
        out = dot(dk_ref[rows, :], wk_ref[...], BY_COLUMNS)
        out = out + dot(dv_ref[rows, :], wv_ref[...], BY_COLUMNS)
        rope = sum_rope[rows, :] * SCALE
        here_rows = pl.ds(side * half, half)
        out = jnp.concatenate([out, rope], axis=1)
        if begun:
            out = out + refs[devices + 5][here_rows, :]
        dlat_ref[here_rows, :] = out.astype(dlat_ref.dtype)


def swap(array, axis, mask):
    size = lax.axis_size(axis)
    return lax.ppermute(array, axis, [(i, i ^ mask) for i in range(size)])


def gather(own, devices):
    far = [own] + [swap(own, "seq", m) for m in range(2, devices, 2)]
    return far + [swap(x, "seq", 1) for x in far]


def join(array, axis, mask):
    return jnp.concatenate([array, swap(array, axis, mask)], axis=0)


def gather_latent(mine, devices):
    step = devices // 2
    while step:
        mine = join(mine, "seq", step)
        step //= 2
    return mine


def gather_by_line(own, mine, me):
    def along(array, pairs):
        return lax.ppermute(
            array, "seq", [(2 * a + y, 2 * b + y) for a, b in pairs for y in range(2)]
        )

    hold = lax.optimization_barrier
    middle = [(1, 2), (2, 1)]
    outward = [(1, 0), (2, 3)]
    place = me // 2
    inner = (place == 1) | (place == 2)
    piece = mine.shape[0]
    mine = join(mine, "seq", 4)
    mine = join(mine, "seq", 2)
    near = swap(own, "seq", 2)
    third = along(own, middle)
    y_own = swap(own, "seq", 1)
    near, third, y_own, mine = hold((near, third, y_own, mine))
    fourth = along(near, middle)
    handed = along(third, outward)
    y_near = swap(near, "seq", 1)
    mine = join(mine, "seq", 1)
    fourth, handed, y_near, mine = hold((fourth, handed, y_near, mine))
    third = jnp.where(inner, third, handed)
    last = along(fourth, outward)
    y_third = swap(third, "seq", 1)
    theirs = swap(mine, "head", 2)
    last, y_third, mine, theirs = hold((last, y_third, mine, theirs))
    fourth = jnp.where(inner, fourth, last)
    fourth, mine, theirs = hold((fourth, mine, theirs))
    y_fourth = swap(fourth, "seq", 1)
    first = lax.axis_index("head") < 2
    mine, theirs = (x.reshape(8, piece, mine.shape[1]) for x in (mine, theirs))
    mine = jnp.concatenate(
        [jnp.where(first, mine, theirs), jnp.where(first, theirs, mine)], axis=1
    ).reshape(16 * piece, mine.shape[2])
    left = place < 2
    places = [place, place ^ 1, jnp.where(left, 2, 1), jnp.where(left, 3, 0)]
    y = me % 2
    sources = [2 * p + y for p in places] + [2 * p + 1 - y for p in places]
    return [own, near, third, fourth, y_own, y_near, y_third, y_fourth], jnp.stack(sources), mine


def shards(queries, latent_rope, w_uk, w_uv, d_out, block_order, block_doc):
    local_rows = queries.shape[0]
    heads = w_uk.shape[1] // NOPE
    devices = lax.axis_size("seq")
    half = local_rows // 2
    total = local_rows * devices
    me = lax.axis_index("seq")
    low = jnp.sum((block_doc[None, :] < block_doc[:, None]).astype(jnp.int32), axis=1)
    low_rows = jnp.repeat(low * half, half).reshape(1, total)

    small = total <= 8 * TILE
    pair = heads if small else 2
    packed = [
        jnp.concatenate(
            [
                queries[:, first * WIDTH : (first + pair) * WIDTH],
                d_out[:, first * VDIM : (first + pair) * VDIM],
            ],
            axis=1,
        )
        for first in range(0, heads, pair)
    ]
    core = lax.axis_index("head") % 2
    where = jnp.stack([me, core]).astype(jnp.int32)
    latent = jnp.pad(latent_rope, ((0, 0), (0, LAT_LANES - D_LAT - ROPE)))
    mine = lax.dynamic_slice_in_dim(latent, core * half, half, axis=0)
    by_line = small and devices == 8 and lax.axis_size("head") == 4
    if by_line:
        mine = lax.dynamic_slice_in_dim(
            mine, lax.axis_index("head") // 2 * (half // 2), half // 2, axis=0
        )
        pieces, sources, mine = gather_by_line(packed[0], mine, me)
        gathered = [pieces]
    else:
        mine = gather_latent(mine, devices)
        gathered = [gather(x, devices) for x in packed]
        order = list(range(0, devices, 2)) + list(range(1, devices, 2))
        sources = jnp.stack([me ^ m for m in order])
    other = swap(mine, "head", 1)

    bf16 = jnp.bfloat16
    mebi = 1024 * 1024

    def params(size):
        return pltpu.CompilerParams(vmem_limit_bytes=(size if small else 60) * mebi)

    keys, values, turned, d_queries = pl.pallas_call(
        functools.partial(project_kernel, devices, half, heads, pair),
        out_shape=(
            jax.ShapeDtypeStruct((heads, total, WIDTH), bf16),
            jax.ShapeDtypeStruct((total, heads * VDIM), bf16),
            jax.ShapeDtypeStruct((D_LAT, total), bf16),
            jax.ShapeDtypeStruct((local_rows, heads * WIDTH), bf16),
        ),
        in_specs=[SMEM, SMEM, SMEM, HBM, HBM, HBM, HBM] + [VMEM] * len(packed),
        out_specs=(VMEM, VMEM, VMEM, VMEM),
        scratch_shapes=[
            pltpu.VMEM((total, LAT_LANES), bf16),
            pltpu.VMEM(w_uk.shape, bf16),
            pltpu.VMEM(w_uv.shape, bf16),
            pltpu.SemaphoreType.DMA((2 * devices,)),
            pltpu.SemaphoreType.DMA((2,)),
        ],
        compiler_params=params(20),
        cost_estimate=pl.CostEstimate(
            flops=20 * 2**30, bytes_accessed=16 * mebi, transcendentals=0
        ),
        name="project",
    )(block_order, low, where, mine, other, w_uk, w_uv, *packed)

    dks, dvs = [], []
    shares = []
    for first in range(0, heads, pair):
        lanes = slice(first * NOPE, (first + pair) * NOPE)
        pieces = gathered[first // pair]
        last = first + pair == heads
        dk, dv, *shares = pl.pallas_call(
            functools.partial(key_kernel, devices, half, pair, len(shares)),
            out_shape=(
                jax.ShapeDtypeStruct((total, pair * NOPE), bf16),
                jax.ShapeDtypeStruct((total, pair * VDIM), bf16),
                jax.ShapeDtypeStruct((local_rows, D_LAT + ROPE), bf16 if last else jnp.float32),
            ),
            in_specs=[SMEM, SMEM, SMEM] + [HBM] * devices + [VMEM] + [HBM] * 4 + [VMEM] * len(shares),
            out_specs=(VMEM, VMEM, VMEM),
            scratch_shapes=[
                pltpu.VMEM((total, pair * (WIDTH + VDIM)), bf16),
                pltpu.VMEM((total, pair * NOPE), jnp.float32),
                pltpu.VMEM((total, pair * VDIM), jnp.float32),
                pltpu.VMEM((total, ROPE), jnp.float32),
                pltpu.SemaphoreType.DMA((2 * devices,)),
                pltpu.VMEM((pair, total, WIDTH), bf16),
                pltpu.VMEM((total, pair * VDIM), bf16),
                pltpu.VMEM((D_LAT, pair * NOPE), bf16),
                pltpu.VMEM((D_LAT, pair * VDIM), bf16),
                pltpu.SemaphoreType.DMA((4,)),
            ],
            compiler_params=params(28),
            cost_estimate=pl.CostEstimate(
                flops=20 * 2**30, bytes_accessed=16 * mebi, transcendentals=0
            ),
            name="keys",
        )(
            low, block_order, sources, *pieces, low_rows,
            keys[first : first + pair], values[:, lanes], w_uk[:, lanes], w_uv[:, lanes], *shares,
        )
        dks.append(dk)
        dvs.append(dv)
    dk = jnp.concatenate(dks, axis=1)
    dv = jnp.concatenate(dvs, axis=1)
    sent = shares[0]
    dlat = sent.astype(jnp.float32) + swap(sent, "head", 1).astype(jnp.float32)
    dlat, dk, dv = lax.optimization_barrier((dlat, dk, dv))
    step = 2
    while step < lax.axis_size("head"):
        sent = dlat.astype(bf16)
        dlat = sent.astype(jnp.float32) + swap(sent, "head", step).astype(jnp.float32)
        step *= 2
    return (d_queries, dlat, dot(turned, dk, BY_ROWS), dot(turned, dv, BY_ROWS))


def solution(mesh):
    return jax.shard_map(
        shards,
        mesh=mesh,
        in_specs=(
            P("seq", "head"),
            P("seq", None),
            P(None, "head"),
            P(None, "head"),
            P("seq", "head"),
            P(),
            P(),
        ),
        out_specs=(P("seq", "head"), P("seq", None), P(None, "head"), P(None, "head")),
        check_vma=False,
    )
```

```python
import functools
import math

import jax
import jax.numpy as jnp
from jax import lax
from jax.experimental import pallas as pl
from jax.experimental.pallas import tpu as pltpu
from jax.sharding import PartitionSpec as P

D_LAT = 512
ROPE = 64
NOPE = 128
VDIM = 128
WIDTH = NOPE + ROPE
SCALE = WIDTH ** (-0.5)
SCALE_LOG2 = SCALE * math.log2(math.e)
NEG_FILL = -1e30
TILE = 256
GRAIN = 128
LAT_LANES = 640
BY_COLUMNS = (((1,), (1,)), ((), ()))
BY_ROWS = (((1,), (0,)), ((), ()))
SMEM = pl.BlockSpec(memory_space=pltpu.SMEM)
VMEM = pl.BlockSpec(memory_space=pltpu.VMEM)
HBM = pl.BlockSpec(memory_space=pl.ANY)


def dot(a, b, dims):
    return lax.dot_general(a, b, dims, preferred_element_type=jnp.float32)


def project_kernel(
    devices, half, heads, pair, resident, order_ref, low_ref, where_ref, mine_ref, other_ref, wk_in, wv_in, *refs
):
    x_refs = refs[: heads // pair]
    keys_ref, values_ref, turned_ref, dq_ref, latent, wk_ref, wv_ref, sem, weight_sem = refs[heads // pair :]
    blocks = 2 * devices
    total = blocks * half
    me, core = where_ref[0], where_ref[1]
    copies = [
        pltpu.make_async_copy(wk_in, wk_ref, weight_sem.at[0]),
        pltpu.make_async_copy(wv_in, wv_ref, weight_sem.at[1]),
    ]
    for copy in copies:
        copy.start()
    masks = [0]
    for bit in reversed(range(devices.bit_length() - 1)):
        masks = masks + [m ^ (1 << bit) for m in masks]
    for number, mask in enumerate(masks):
        for side, source in enumerate((mine_ref, other_ref)):
            block = order_ref[2 * (me ^ mask) + (core ^ side)]
            rows = pl.ds(pl.multiple_of(block * half, 16), half)
            from_rows = pl.ds(number * half, half)
            if resident:
                latent[rows, :] = source[from_rows, :]
                continue
            copy = pltpu.make_async_copy(
                source.at[from_rows, :], latent.at[rows, :], sem.at[2 * number + side]
            )
            copy.start()
            copies.append(copy)
    for copy in copies:
        copy.wait()
    for first in range(0, total, TILE):
        rows = pl.ds(first, TILE)
        part = latent[rows, :D_LAT]
        rope = latent[rows, D_LAT : D_LAT + ROPE]
        up_keys = dot(part, wk_ref[...], BY_ROWS).astype(jnp.bfloat16)
        for head in range(heads):
            keys_ref[head, rows, :] = jnp.concatenate(
                [up_keys[:, head * NOPE : (head + 1) * NOPE], rope], axis=1
            )
        values_ref[rows, :] = dot(part, wv_ref[...], BY_ROWS).astype(jnp.bfloat16)
        turned_ref[:, first : first + TILE] = part.T
    span = (blocks // 2) * half
    grad_at = pair * WIDTH
    for side in range(2):
        block = order_ref[2 * me + side]
        start = pl.multiple_of(jnp.maximum(block - (blocks // 2 - 1), 0) * half, 16)
        window = pl.ds(start, span)
        key_pos = start + lax.broadcasted_iota(jnp.int32, (half, span), 1)
        query_pos = block * half + lax.broadcasted_iota(jnp.int32, (half, span), 0)
        seen = (key_pos <= query_pos) & (key_pos >= low_ref[block] * half)
        bias = jnp.where(seen, 0.0, NEG_FILL)
        rows = pl.ds(side * half, half)
        outs = []
        for head in range(heads):
            x_ref, at = x_refs[head // pair], head % pair
            query = x_ref[rows, at * WIDTH : (at + 1) * WIDTH]
            grad = x_ref[rows, grad_at + at * VDIM : grad_at + (at + 1) * VDIM]
            keys = keys_ref[head, window, :]
            values = values_ref[window, head * VDIM : (head + 1) * VDIM]
            scores = dot(query, keys, BY_COLUMNS) * SCALE_LOG2 + bias
            expo = jnp.exp2(scores - jnp.max(scores, axis=1, keepdims=True))
            probs = expo * (1.0 / jnp.sum(expo, axis=1, keepdims=True))
            grad_probs = dot(grad, values, BY_COLUMNS)
            delta = jnp.sum(probs * grad_probs, axis=1, keepdims=True)
            grad_scores = (probs * (grad_probs - delta) * SCALE).astype(jnp.bfloat16)
            outs.append(dot(grad_scores, keys, BY_ROWS).astype(jnp.bfloat16))
        dq_ref[rows, :] = jnp.concatenate(outs, axis=1)


def key_kernel(devices, half, here, begun, resident, low_ref, order_ref, source_ref, *refs):
    x_refs = refs[:devices]
    low_rows_ref, keys_ref, values_ref, wk_ref, wv_ref = refs[devices : devices + 5]
    dk_ref, dv_ref, dlat_ref = refs[devices + 5 + begun : devices + 8 + begun]
    x_all, sum_nope, sum_value, sum_rope, sem = refs[devices + 8 + begun :]
    blocks = 2 * devices
    total = blocks * half
    grad_at = here * WIDTH
    copies = []
    for number in range(devices):
        for side in range(2):
            block = order_ref[2 * source_ref[number] + side]
            rows = pl.ds(pl.multiple_of(block * half, 16), half)
            from_rows = pl.ds(side * half, half)
            if resident:
                x_all[rows, :] = x_refs[number][from_rows, :]
                continue
            copy = pltpu.make_async_copy(
                x_refs[number].at[from_rows, :], x_all.at[rows, :], sem.at[2 * number + side]
            )
            copy.start()
            copies.append(copy)
    sum_nope[...] = jnp.zeros_like(sum_nope)
    sum_value[...] = jnp.zeros_like(sum_value)
    sum_rope[...] = jnp.zeros_like(sum_rope)
    for copy in copies:
        copy.wait()

    def tile(first, start, span):
        window = pl.ds(start, span)
        rows = pl.ds(first, TILE)
        key_pos = start + lax.broadcasted_iota(jnp.int32, (span, TILE), 0)
        query_pos = first + lax.broadcasted_iota(jnp.int32, (span, TILE), 1)
        seen = (key_pos <= query_pos) & (key_pos >= low_rows_ref[:, rows])
        bias = jnp.where(seen, 0.0, NEG_FILL)
        def begin(head):
            lanes = slice(head * NOPE, (head + 1) * NOPE)
            query = x_all[rows, head * WIDTH : (head + 1) * WIDTH]
            grad = x_all[rows, grad_at + head * VDIM : grad_at + (head + 1) * VDIM]
            scores = dot(keys_ref[head, window, :], query, BY_COLUMNS)
            return lanes, query, grad, scores, dot(values_ref[window, lanes], grad, BY_COLUMNS)

        def middle(lanes, query, grad, scores, grad_probs):
            scores = scores * SCALE_LOG2 + bias
            expo = jnp.exp2(scores - jnp.max(scores, axis=0, keepdims=True))
            inverse = 1.0 / jnp.sum(expo, axis=0, keepdims=True)
            delta = jnp.sum(expo * grad_probs, axis=0, keepdims=True) * inverse
            probs = expo * inverse
            grad_scores = (probs * (grad_probs - delta)).astype(jnp.bfloat16)
            return lanes, query, grad, probs.astype(jnp.bfloat16), grad_scores

        def end(lanes, query, grad, probs, grad_scores):
            sum_value[window, lanes] += dot(probs, grad, BY_ROWS)
            key_grad = dot(grad_scores, query, BY_ROWS)
            sum_nope[window, lanes] += key_grad[:, :NOPE]
            return key_grad[:, NOPE:]

        rope = 0.0
        begun_heads = [begin(0)]
        for head in range(here):
            if head + 1 < here:
                begun_heads.append(begin(head + 1))
            rope = rope + end(*middle(*begun_heads[head]))
        sum_rope[window, :] += rope

    def step(number, carry):
        first = pl.multiple_of(number * TILE, TILE)
        oldest = low_ref[first // half] * half
        need = (first + TILE - oldest + GRAIN - 1) // GRAIN
        for size in sizes:
            below = sizes[sizes.index(size) - 1] if size != sizes[0] else 0

            @pl.when((need <= size) & (need > below))
            def _(size=size):
                start = jnp.maximum(first + TILE - size * GRAIN, 0)
                tile(first, pl.multiple_of(start, 16), size * GRAIN)

        return carry

    most = -(-(devices * half + TILE) // GRAIN)
    sizes = list(range(TILE // GRAIN, most + 1, max(1, most // 8)))
    if sizes[-1] != most:
        sizes.append(most)
    lax.fori_loop(0, total // TILE, step, 0)
    dk_ref[...] = (sum_nope[...] * SCALE).astype(jnp.bfloat16)
    dv_ref[...] = sum_value[...].astype(jnp.bfloat16)
    own = []
    for side in range(2):
        block = order_ref[2 * source_ref[0] + side]
        own.append(pl.ds(pl.multiple_of(block * half, 16), half))

    def take(ref):
        return jnp.concatenate([ref[rows, :] for rows in own], axis=0)

    out = dot(take(dk_ref), wk_ref[...], BY_COLUMNS) + dot(take(dv_ref), wv_ref[...], BY_COLUMNS)
    out = jnp.concatenate([out, take(sum_rope) * SCALE], axis=1)
    if begun:
        out = out + refs[devices + 5][...]
    dlat_ref[...] = out.astype(dlat_ref.dtype)


def swap(array, axis, mask):
    size = lax.axis_size(axis)
    return lax.ppermute(array, axis, [(i, i ^ mask) for i in range(size)])


def gather(own, devices):
    far = [own] + [swap(own, "seq", m) for m in range(2, devices, 2)]
    return far + [swap(x, "seq", 1) for x in far]


def join(array, axis, mask):
    return jnp.concatenate([array, swap(array, axis, mask)], axis=0)


def gather_latent(mine, devices):
    step = devices // 2
    while step:
        mine = join(mine, "seq", step)
        step //= 2
    return mine


def gather_by_line(own, mine, me):
    def along(array, pairs):
        return lax.ppermute(
            array, "seq", [(2 * a + y, 2 * b + y) for a, b in pairs for y in range(2)]
        )

    hold = lax.optimization_barrier
    middle = [(1, 2), (2, 1)]
    outward = [(1, 0), (2, 3)]
    place = me // 2
    inner = (place == 1) | (place == 2)
    piece = mine.shape[0]
    mine = jnp.concatenate([mine] + [swap(mine, "seq", mask) for mask in (4, 2, 6)], axis=0)
    own, mine = hold((own, mine))
    near = swap(own, "seq", 2)
    third = along(own, middle)
    y_own = swap(own, "seq", 1)
    near, third, y_own = hold((near, third, y_own))
    fourth = along(near, middle)
    handed = along(third, outward)
    y_near = swap(near, "seq", 1)
    mine = join(mine, "seq", 1)
    fourth, handed, y_near, mine = hold((fourth, handed, y_near, mine))
    third = jnp.where(inner, third, handed)
    last = along(fourth, outward)
    y_third = swap(third, "seq", 1)
    theirs = swap(mine, "head", 2)
    first = lax.axis_index("head") < 2
    mine, theirs = (x.reshape(8, piece, mine.shape[1]) for x in (mine, theirs))
    mine = jnp.concatenate(
        [jnp.where(first, mine, theirs), jnp.where(first, theirs, mine)], axis=1
    ).reshape(16 * piece, mine.shape[2])
    last, y_third, mine = hold((last, y_third, mine))
    fourth = jnp.where(inner, fourth, last)
    fourth, mine = hold((fourth, mine))
    y_fourth = swap(fourth, "seq", 1)
    left = place < 2
    places = [place, place ^ 1, jnp.where(left, 2, 1), jnp.where(left, 3, 0)]
    y = me % 2
    sources = [2 * p + y for p in places] + [2 * p + 1 - y for p in places]
    return [own, near, third, fourth, y_own, y_near, y_third, y_fourth], jnp.stack(sources), mine


def shards(queries, latent_rope, w_uk, w_uv, d_out, block_order, block_doc):
    local_rows = queries.shape[0]
    heads = w_uk.shape[1] // NOPE
    devices = lax.axis_size("seq")
    half = local_rows // 2
    total = local_rows * devices
    me = lax.axis_index("seq")
    low = jnp.sum((block_doc[None, :] < block_doc[:, None]).astype(jnp.int32), axis=1)
    low_rows = jnp.repeat(low * half, half).reshape(1, total)

    small = total <= 8 * TILE
    pair = heads if small else 2
    packed = [
        jnp.concatenate(
            [
                queries[:, first * WIDTH : (first + pair) * WIDTH],
                d_out[:, first * VDIM : (first + pair) * VDIM],
            ],
            axis=1,
        )
        for first in range(0, heads, pair)
    ]
    core = lax.axis_index("head") % 2
    where = jnp.stack([me, core]).astype(jnp.int32)
    latent = jnp.pad(latent_rope, ((0, 0), (0, LAT_LANES - D_LAT - ROPE)))
    mine = lax.dynamic_slice_in_dim(latent, core * half, half, axis=0)
    by_line = small and devices == 8 and lax.axis_size("head") == 4
    if by_line:
        mine = lax.dynamic_slice_in_dim(
            mine, lax.axis_index("head") // 2 * (half // 2), half // 2, axis=0
        )
        pieces, sources, mine = gather_by_line(packed[0], mine, me)
        gathered = [pieces]
    else:
        mine = gather_latent(mine, devices)
        gathered = [gather(x, devices) for x in packed]
        order = list(range(0, devices, 2)) + list(range(1, devices, 2))
        sources = jnp.stack([me ^ m for m in order])
    other = swap(mine, "head", 1)

    bf16 = jnp.bfloat16
    mebi = 1024 * 1024

    def params(size):
        return pltpu.CompilerParams(vmem_limit_bytes=(size if small else 60) * mebi)

    keys, values, turned, d_queries = pl.pallas_call(
        functools.partial(project_kernel, devices, half, heads, pair, small),
        out_shape=(
            jax.ShapeDtypeStruct((heads, total, WIDTH), bf16),
            jax.ShapeDtypeStruct((total, heads * VDIM), bf16),
            jax.ShapeDtypeStruct((D_LAT, total), bf16),
            jax.ShapeDtypeStruct((local_rows, heads * WIDTH), bf16),
        ),
        in_specs=[SMEM, SMEM, SMEM] + [VMEM if small else HBM] * 2 + [HBM, HBM] + [VMEM] * len(packed),
        out_specs=(VMEM, VMEM, VMEM, VMEM),
        scratch_shapes=[
            pltpu.VMEM((total, LAT_LANES), bf16),
            pltpu.VMEM(w_uk.shape, bf16),
            pltpu.VMEM(w_uv.shape, bf16),
            pltpu.SemaphoreType.DMA((2 * devices,)),
            pltpu.SemaphoreType.DMA((2,)),
        ],
        compiler_params=params(20),
        cost_estimate=pl.CostEstimate(
            flops=20 * 2**30, bytes_accessed=16 * mebi, transcendentals=0
        ),
        name="project",
    )(block_order, low, where, mine, other, w_uk, w_uv, *packed)

    dks, dvs = [], []
    shares = []
    for first in range(0, heads, pair):
        lanes = slice(first * NOPE, (first + pair) * NOPE)
        pieces = gathered[first // pair]
        last = first + pair == heads
        dk, dv, *shares = pl.pallas_call(
            functools.partial(key_kernel, devices, half, pair, len(shares), small),
            out_shape=(
                jax.ShapeDtypeStruct((total, pair * NOPE), bf16),
                jax.ShapeDtypeStruct((total, pair * VDIM), bf16),
                jax.ShapeDtypeStruct((local_rows, D_LAT + ROPE), bf16 if last else jnp.float32),
            ),
            in_specs=[SMEM, SMEM, SMEM] + [VMEM if small else HBM] * devices + [VMEM] * (5 + len(shares)),
            out_specs=(VMEM, VMEM, VMEM),
            scratch_shapes=[
                pltpu.VMEM((total, pair * (WIDTH + VDIM)), bf16),
                pltpu.VMEM((total, pair * NOPE), jnp.float32),
                pltpu.VMEM((total, pair * VDIM), jnp.float32),
                pltpu.VMEM((total, ROPE), jnp.float32),
                pltpu.SemaphoreType.DMA((2 * devices,)),
            ],
            compiler_params=params(28),
            cost_estimate=pl.CostEstimate(
                flops=20 * 2**30, bytes_accessed=16 * mebi, transcendentals=0
            ),
            name="keys",
        )(
            low, block_order, sources, *pieces, low_rows,
            keys[first : first + pair], values[:, lanes], w_uk[:, lanes], w_uv[:, lanes], *shares,
        )
        dks.append(dk)
        dvs.append(dv)
    dk = jnp.concatenate(dks, axis=1)
    dv = jnp.concatenate(dvs, axis=1)
    sent = shares[0]
    dlat = sent.astype(jnp.float32) + swap(sent, "head", 1).astype(jnp.float32)
    dlat, dk, dv = lax.optimization_barrier((dlat, dk, dv))
    step = 2
    while step < lax.axis_size("head"):
        sent = dlat.astype(bf16)
        dlat = sent.astype(jnp.float32) + swap(sent, "head", step).astype(jnp.float32)
        step *= 2
    return (d_queries, dlat, dot(turned, dk, BY_ROWS), dot(turned, dv, BY_ROWS))


def solution(mesh):
    return jax.shard_map(
        shards,
        mesh=mesh,
        in_specs=(
            P("seq", "head"),
            P("seq", None),
            P(None, "head"),
            P(None, "head"),
            P("seq", "head"),
            P(),
            P(),
        ),
        out_specs=(P("seq", "head"), P("seq", None), P(None, "head"), P(None, "head")),
        check_vma=False,
    )
```

```python
import functools
import math

import jax
import jax.numpy as jnp
from jax import lax
from jax.experimental import pallas as pl
from jax.experimental.pallas import tpu as pltpu
from jax.sharding import PartitionSpec as P

D_LAT = 512
ROPE = 64
NOPE = 128
VDIM = 128
WIDTH = NOPE + ROPE
SCALE = WIDTH ** (-0.5)
SCALE_LOG2 = SCALE * math.log2(math.e)
NEG_FILL = -1e30
TILE = 256
GRAIN = 128
LAT_LANES = 640
BY_COLUMNS = (((1,), (1,)), ((), ()))
BY_ROWS = (((1,), (0,)), ((), ()))
SMEM = pl.BlockSpec(memory_space=pltpu.SMEM)
VMEM = pl.BlockSpec(memory_space=pltpu.VMEM)
HBM = pl.BlockSpec(memory_space=pl.ANY)


def dot(a, b, dims):
    return lax.dot_general(a, b, dims, preferred_element_type=jnp.float32)


def project_kernel(
    devices, half, heads, pair, resident, order_ref, low_ref, where_ref, mine_ref, other_ref, wk_in, wv_in, *refs
):
    x_refs = refs[: heads // pair]
    keys_ref, values_ref, turned_ref, dq_ref, latent, wk_ref, wv_ref, sem, weight_sem = refs[heads // pair :]
    blocks = 2 * devices
    total = blocks * half
    me, core = where_ref[0], where_ref[1]
    copies = [
        pltpu.make_async_copy(wk_in, wk_ref, weight_sem.at[0]),
        pltpu.make_async_copy(wv_in, wv_ref, weight_sem.at[1]),
    ]
    for copy in copies:
        copy.start()
    masks = [0]
    for bit in reversed(range(devices.bit_length() - 1)):
        masks = masks + [m ^ (1 << bit) for m in masks]
    for number, mask in enumerate(masks):
        for side, source in enumerate((mine_ref, other_ref)):
            block = order_ref[2 * (me ^ mask) + (core ^ side)]
            rows = pl.ds(pl.multiple_of(block * half, 16), half)
            from_rows = pl.ds(number * half, half)
            if resident:
                latent[rows, :] = source[from_rows, :]
                continue
            copy = pltpu.make_async_copy(
                source.at[from_rows, :], latent.at[rows, :], sem.at[2 * number + side]
            )
            copy.start()
            copies.append(copy)
    for copy in copies:
        copy.wait()
    for first in range(0, total, TILE):
        rows = pl.ds(first, TILE)
        part = latent[rows, :D_LAT]
        rope = latent[rows, D_LAT : D_LAT + ROPE]
        up_keys = dot(part, wk_ref[...], BY_ROWS).astype(jnp.bfloat16)
        for head in range(heads):
            keys_ref[head, rows, :] = jnp.concatenate(
                [up_keys[:, head * NOPE : (head + 1) * NOPE], rope], axis=1
            )
        values_ref[rows, :] = dot(part, wv_ref[...], BY_ROWS).astype(jnp.bfloat16)
        turned_ref[:, first : first + TILE] = part.T
    span = (blocks // 2) * half
    grad_at = pair * WIDTH
    for side in range(2):
        block = order_ref[2 * me + side]
        start = pl.multiple_of(jnp.maximum(block - (blocks // 2 - 1), 0) * half, 16)
        window = pl.ds(start, span)
        key_pos = start + lax.broadcasted_iota(jnp.int32, (half, span), 1)
        query_pos = block * half + lax.broadcasted_iota(jnp.int32, (half, span), 0)
        seen = (key_pos <= query_pos) & (key_pos >= low_ref[block] * half)
        bias = jnp.where(seen, 0.0, NEG_FILL)
        rows = pl.ds(side * half, half)
        outs = []
        for head in range(heads):
            x_ref, at = x_refs[head // pair], head % pair
            query = x_ref[rows, at * WIDTH : (at + 1) * WIDTH]
            grad = x_ref[rows, grad_at + at * VDIM : grad_at + (at + 1) * VDIM]
            keys = keys_ref[head, window, :]
            values = values_ref[window, head * VDIM : (head + 1) * VDIM]
            scores = dot(query, keys, BY_COLUMNS) * SCALE_LOG2 + bias
            expo = jnp.exp2(scores - jnp.max(scores, axis=1, keepdims=True))
            probs = expo * (1.0 / jnp.sum(expo, axis=1, keepdims=True))
            grad_probs = dot(grad, values, BY_COLUMNS)
            delta = jnp.sum(probs * grad_probs, axis=1, keepdims=True)
            grad_scores = (probs * (grad_probs - delta) * SCALE).astype(jnp.bfloat16)
            outs.append(dot(grad_scores, keys, BY_ROWS).astype(jnp.bfloat16))
        dq_ref[rows, :] = jnp.concatenate(outs, axis=1)


def key_kernel(devices, half, here, begun, resident, low_ref, order_ref, source_ref, *refs):
    x_refs = refs[:devices]
    low_rows_ref, keys_ref, values_ref, wk_ref, wv_ref = refs[devices : devices + 5]
    dk_ref, dv_ref, dlat_ref = refs[devices + 5 + begun : devices + 8 + begun]
    x_all, sum_nope, sum_value, sum_rope, sem = refs[devices + 8 + begun :]
    blocks = 2 * devices
    total = blocks * half
    grad_at = here * WIDTH
    copies = []
    for number in range(devices):
        for side in range(2):
            block = order_ref[2 * source_ref[number] + side]
            rows = pl.ds(pl.multiple_of(block * half, 16), half)
            from_rows = pl.ds(side * half, half)
            if resident:
                x_all[rows, :] = x_refs[number][from_rows, :]
                continue
            copy = pltpu.make_async_copy(
                x_refs[number].at[from_rows, :], x_all.at[rows, :], sem.at[2 * number + side]
            )
            copy.start()
            copies.append(copy)
    sum_nope[...] = jnp.zeros_like(sum_nope)
    sum_value[...] = jnp.zeros_like(sum_value)
    sum_rope[...] = jnp.zeros_like(sum_rope)
    for copy in copies:
        copy.wait()

    def tile(first, start, span):
        window = pl.ds(start, span)
        rows = pl.ds(first, TILE)
        key_pos = start + lax.broadcasted_iota(jnp.int32, (span, TILE), 0)
        query_pos = first + lax.broadcasted_iota(jnp.int32, (span, TILE), 1)
        seen = (key_pos <= query_pos) & (key_pos >= low_rows_ref[:, rows])
        bias = jnp.where(seen, 0.0, NEG_FILL)
        def begin(head):
            lanes = slice(head * NOPE, (head + 1) * NOPE)
            query = x_all[rows, head * WIDTH : (head + 1) * WIDTH]
            grad = x_all[rows, grad_at + head * VDIM : grad_at + (head + 1) * VDIM]
            scores = dot(keys_ref[head, window, :], query, BY_COLUMNS)
            return lanes, query, grad, scores, dot(values_ref[window, lanes], grad, BY_COLUMNS)

        def middle(lanes, query, grad, scores, grad_probs):
            scores = scores * SCALE_LOG2 + bias
            expo = jnp.exp2(scores - jnp.max(scores, axis=0, keepdims=True))
            inverse = 1.0 / jnp.sum(expo, axis=0, keepdims=True)
            delta = jnp.sum(expo * grad_probs, axis=0, keepdims=True) * inverse
            probs = expo * inverse
            grad_scores = (probs * (grad_probs - delta)).astype(jnp.bfloat16)
            return lanes, query, grad, probs.astype(jnp.bfloat16), grad_scores

        def end(lanes, query, grad, probs, grad_scores):
            sum_value[window, lanes] += dot(probs, grad, BY_ROWS)
            key_grad = dot(grad_scores, query, BY_ROWS)
            sum_nope[window, lanes] += key_grad[:, :NOPE]
            return key_grad[:, NOPE:]

        rope = 0.0
        begun_heads = [begin(0)]
        for head in range(here):
            if head + 1 < here:
                begun_heads.append(begin(head + 1))
            rope = rope + end(*middle(*begun_heads[head]))
        sum_rope[window, :] += rope

    def step(number, carry):
        first = pl.multiple_of(number * TILE, TILE)
        oldest = low_ref[first // half] * half
        need = (first + TILE - oldest + GRAIN - 1) // GRAIN
        for size in sizes:
            below = sizes[sizes.index(size) - 1] if size != sizes[0] else 0

            @pl.when((need <= size) & (need > below))
            def _(size=size):
                start = jnp.maximum(first + TILE - size * GRAIN, 0)
                tile(first, pl.multiple_of(start, 16), size * GRAIN)

        return carry

    most = -(-(devices * half + TILE) // GRAIN)
    sizes = list(range(TILE // GRAIN, most + 1, max(1, most // 8)))
    if sizes[-1] != most:
        sizes.append(most)
    lax.fori_loop(0, total // TILE, step, 0)
    dk_ref[...] = (sum_nope[...] * SCALE).astype(jnp.bfloat16)
    dv_ref[...] = sum_value[...].astype(jnp.bfloat16)
    own = []
    for side in range(2):
        block = order_ref[2 * source_ref[0] + side]
        own.append(pl.ds(pl.multiple_of(block * half, 16), half))

    def take(ref):
        return jnp.concatenate([ref[rows, :] for rows in own], axis=0)

    out = dot(take(dk_ref), wk_ref[...], BY_COLUMNS) + dot(take(dv_ref), wv_ref[...], BY_COLUMNS)
    out = jnp.concatenate([out, take(sum_rope) * SCALE], axis=1)
    if begun:
        out = out + refs[devices + 5][...]
    dlat_ref[...] = out.astype(dlat_ref.dtype)


def swap(array, axis, mask):
    size = lax.axis_size(axis)
    return lax.ppermute(array, axis, [(i, i ^ mask) for i in range(size)])


def gather(own, devices):
    far = [own] + [swap(own, "seq", m) for m in range(2, devices, 2)]
    return far + [swap(x, "seq", 1) for x in far]


def join(array, axis, mask):
    return jnp.concatenate([array, swap(array, axis, mask)], axis=0)


def gather_latent(mine, devices):
    step = devices // 2
    while step:
        mine = join(mine, "seq", step)
        step //= 2
    return mine


def gather_by_line(own, mine, me):
    def along(array, pairs):
        return lax.ppermute(
            array, "seq", [(2 * a + y, 2 * b + y) for a, b in pairs for y in range(2)]
        )

    hold = lax.optimization_barrier
    middle = [(1, 2), (2, 1)]
    outward = [(1, 0), (2, 3)]
    place = me // 2
    inner = (place == 1) | (place == 2)
    piece = mine.shape[0]
    mine = jnp.concatenate([mine] + [swap(mine, "seq", mask) for mask in (4, 2, 6)], axis=0)
    own, mine = hold((own, mine))
    near = swap(own, "seq", 2)
    third = along(own, middle)
    y_own = swap(own, "seq", 1)
    mine = join(mine, "seq", 1)
    near, third, y_own, mine = hold((near, third, y_own, mine))
    fourth = along(near, middle)
    handed = along(third, outward)
    y_near = swap(near, "seq", 1)
    theirs = swap(mine, "head", 2)
    fourth, handed, y_near, mine, theirs = hold((fourth, handed, y_near, mine, theirs))
    third = jnp.where(inner, third, handed)
    last = along(fourth, outward)
    y_third = swap(third, "seq", 1)
    first = lax.axis_index("head") < 2
    mine, theirs = (x.reshape(8, piece, mine.shape[1]) for x in (mine, theirs))
    mine = jnp.concatenate(
        [jnp.where(first, mine, theirs), jnp.where(first, theirs, mine)], axis=1
    ).reshape(16 * piece, mine.shape[2])
    other = swap(mine, "head", 1)
    last, y_third = hold((last, y_third))
    fourth = jnp.where(inner, fourth, last)
    y_fourth = swap(fourth, "seq", 1)
    left = place < 2
    places = [place, place ^ 1, jnp.where(left, 2, 1), jnp.where(left, 3, 0)]
    y = me % 2
    sources = [2 * p + y for p in places] + [2 * p + 1 - y for p in places]
    return [own, near, third, fourth, y_own, y_near, y_third, y_fourth], jnp.stack(sources), mine, other


def shards(queries, latent_rope, w_uk, w_uv, d_out, block_order, block_doc):
    local_rows = queries.shape[0]
    heads = w_uk.shape[1] // NOPE
    devices = lax.axis_size("seq")
    half = local_rows // 2
    total = local_rows * devices
    me = lax.axis_index("seq")
    low = jnp.sum((block_doc[None, :] < block_doc[:, None]).astype(jnp.int32), axis=1)
    low_rows = jnp.repeat(low * half, half).reshape(1, total)

    small = total <= 8 * TILE
    pair = heads if small else 2
    packed = [
        jnp.concatenate(
            [
                queries[:, first * WIDTH : (first + pair) * WIDTH],
                d_out[:, first * VDIM : (first + pair) * VDIM],
            ],
            axis=1,
        )
        for first in range(0, heads, pair)
    ]
    core = lax.axis_index("head") % 2
    where = jnp.stack([me, core]).astype(jnp.int32)
    latent = jnp.pad(latent_rope, ((0, 0), (0, LAT_LANES - D_LAT - ROPE)))
    mine = lax.dynamic_slice_in_dim(latent, core * half, half, axis=0)
    by_line = small and devices == 8 and lax.axis_size("head") == 4
    if by_line:
        mine = lax.dynamic_slice_in_dim(
            mine, lax.axis_index("head") // 2 * (half // 2), half // 2, axis=0
        )
        pieces, sources, mine, other = gather_by_line(packed[0], mine, me)
        gathered = [pieces]
    else:
        mine = gather_latent(mine, devices)
        gathered = [gather(x, devices) for x in packed]
        order = list(range(0, devices, 2)) + list(range(1, devices, 2))
        sources = jnp.stack([me ^ m for m in order])
        other = swap(mine, "head", 1)

    bf16 = jnp.bfloat16
    mebi = 1024 * 1024

    def params(size):
        return pltpu.CompilerParams(vmem_limit_bytes=(size if small else 60) * mebi)

    keys, values, turned, d_queries = pl.pallas_call(
        functools.partial(project_kernel, devices, half, heads, pair, small),
        out_shape=(
            jax.ShapeDtypeStruct((heads, total, WIDTH), bf16),
            jax.ShapeDtypeStruct((total, heads * VDIM), bf16),
            jax.ShapeDtypeStruct((D_LAT, total), bf16),
            jax.ShapeDtypeStruct((local_rows, heads * WIDTH), bf16),
        ),
        in_specs=[SMEM, SMEM, SMEM] + [VMEM if small else HBM] * 2 + [HBM, HBM] + [VMEM] * len(packed),
        out_specs=(VMEM, VMEM, VMEM, VMEM),
        scratch_shapes=[
            pltpu.VMEM((total, LAT_LANES), bf16),
            pltpu.VMEM(w_uk.shape, bf16),
            pltpu.VMEM(w_uv.shape, bf16),
            pltpu.SemaphoreType.DMA((2 * devices,)),
            pltpu.SemaphoreType.DMA((2,)),
        ],
        compiler_params=params(20),
        cost_estimate=pl.CostEstimate(
            flops=20 * 2**30, bytes_accessed=16 * mebi, transcendentals=0
        ),
        name="project",
    )(block_order, low, where, mine, other, w_uk, w_uv, *packed)

    dks, dvs = [], []
    shares = []
    for first in range(0, heads, pair):
        lanes = slice(first * NOPE, (first + pair) * NOPE)
        pieces = gathered[first // pair]
        last = first + pair == heads
        dk, dv, *shares = pl.pallas_call(
            functools.partial(key_kernel, devices, half, pair, len(shares), small),
            out_shape=(
                jax.ShapeDtypeStruct((total, pair * NOPE), bf16),
                jax.ShapeDtypeStruct((total, pair * VDIM), bf16),
                jax.ShapeDtypeStruct((local_rows, D_LAT + ROPE), bf16 if last else jnp.float32),
            ),
            in_specs=[SMEM, SMEM, SMEM] + [VMEM if small else HBM] * devices + [VMEM] * (5 + len(shares)),
            out_specs=(VMEM, VMEM, VMEM),
            scratch_shapes=[
                pltpu.VMEM((total, pair * (WIDTH + VDIM)), bf16),
                pltpu.VMEM((total, pair * NOPE), jnp.float32),
                pltpu.VMEM((total, pair * VDIM), jnp.float32),
                pltpu.VMEM((total, ROPE), jnp.float32),
                pltpu.SemaphoreType.DMA((2 * devices,)),
            ],
            compiler_params=params(28),
            cost_estimate=pl.CostEstimate(
                flops=20 * 2**30, bytes_accessed=16 * mebi, transcendentals=0
            ),
            name="keys",
        )(
            low, block_order, sources, *pieces, low_rows,
            keys[first : first + pair], values[:, lanes], w_uk[:, lanes], w_uv[:, lanes], *shares,
        )
        dks.append(dk)
        dvs.append(dv)
    dk = jnp.concatenate(dks, axis=1)
    dv = jnp.concatenate(dvs, axis=1)
    sent = shares[0]
    dlat = sent.astype(jnp.float32) + swap(sent, "head", 1).astype(jnp.float32)
    dlat, dk, dv = lax.optimization_barrier((dlat, dk, dv))
    step = 2
    while step < lax.axis_size("head"):
        sent = dlat.astype(bf16)
        dlat = sent.astype(jnp.float32) + swap(sent, "head", step).astype(jnp.float32)
        step *= 2
    return (d_queries, dlat, dot(turned, dk, BY_ROWS), dot(turned, dv, BY_ROWS))


def solution(mesh):
    return jax.shard_map(
        shards,
        mesh=mesh,
        in_specs=(
            P("seq", "head"),
            P("seq", None),
            P(None, "head"),
            P(None, "head"),
            P("seq", "head"),
            P(),
            P(),
        ),
        out_specs=(P("seq", "head"), P("seq", None), P(None, "head"), P(None, "head")),
        check_vma=False,
    )
```

```python
import functools
import math

import jax
import jax.numpy as jnp
from jax import lax
from jax.experimental import pallas as pl
from jax.experimental.pallas import tpu as pltpu
from jax.sharding import PartitionSpec as P

D_LAT = 512
ROPE = 64
NOPE = 128
VDIM = 128
WIDTH = NOPE + ROPE
SCALE = WIDTH ** (-0.5)
SCALE_LOG2 = SCALE * math.log2(math.e)
NEG_FILL = -1e30
TILE = 256
GRAIN = 128
LAT_LANES = 640
BY_COLUMNS = (((1,), (1,)), ((), ()))
BY_ROWS = (((1,), (0,)), ((), ()))
SMEM = pl.BlockSpec(memory_space=pltpu.SMEM)
VMEM = pl.BlockSpec(memory_space=pltpu.VMEM)
HBM = pl.BlockSpec(memory_space=pl.ANY)


def dot(a, b, dims):
    return lax.dot_general(a, b, dims, preferred_element_type=jnp.float32)


def project_kernel(
    devices, half, heads, pair, resident, order_ref, low_ref, where_ref, mine_ref, other_ref, wk_in, wv_in, *refs
):
    x_refs = refs[: heads // pair]
    keys_ref, values_ref, turned_ref, dq_ref, latent, wk_ref, wv_ref, sem, weight_sem = refs[heads // pair :]
    blocks = 2 * devices
    total = blocks * half
    me, core = where_ref[0], where_ref[1]
    copies = [
        pltpu.make_async_copy(wk_in, wk_ref, weight_sem.at[0]),
        pltpu.make_async_copy(wv_in, wv_ref, weight_sem.at[1]),
    ]
    for copy in copies:
        copy.start()
    masks = [0]
    for bit in reversed(range(devices.bit_length() - 1)):
        masks = masks + [m ^ (1 << bit) for m in masks]
    for number, mask in enumerate(masks):
        for side, source in enumerate((mine_ref, other_ref)):
            block = order_ref[2 * (me ^ mask) + (core ^ side)]
            rows = pl.ds(pl.multiple_of(block * half, 16), half)
            from_rows = pl.ds(number * half, half)
            if resident:
                latent[rows, :] = source[from_rows, :]
                continue
            copy = pltpu.make_async_copy(
                source.at[from_rows, :], latent.at[rows, :], sem.at[2 * number + side]
            )
            copy.start()
            copies.append(copy)
    for copy in copies:
        copy.wait()
    for first in range(0, total, TILE):
        rows = pl.ds(first, TILE)
        part = latent[rows, :D_LAT]
        rope = latent[rows, D_LAT : D_LAT + ROPE]
        up_keys = dot(part, wk_ref[...], BY_ROWS).astype(jnp.bfloat16)
        for head in range(heads):
            keys_ref[head, rows, :] = jnp.concatenate(
                [up_keys[:, head * NOPE : (head + 1) * NOPE], rope], axis=1
            )
        values_ref[rows, :] = dot(part, wv_ref[...], BY_ROWS).astype(jnp.bfloat16)
        turned_ref[:, first : first + TILE] = part.T
    span = (blocks // 2) * half
    grad_at = pair * WIDTH
    for side in range(2):
        block = order_ref[2 * me + side]
        start = pl.multiple_of(jnp.maximum(block - (blocks // 2 - 1), 0) * half, 16)
        window = pl.ds(start, span)
        key_pos = start + lax.broadcasted_iota(jnp.int32, (half, span), 1)
        query_pos = block * half + lax.broadcasted_iota(jnp.int32, (half, span), 0)
        seen = (key_pos <= query_pos) & (key_pos >= low_ref[block] * half)
        bias = jnp.where(seen, 0.0, NEG_FILL)
        rows = pl.ds(side * half, half)
        outs = []
        for head in range(heads):
            x_ref, at = x_refs[head // pair], head % pair
            query = x_ref[rows, at * WIDTH : (at + 1) * WIDTH]
            grad = x_ref[rows, grad_at + at * VDIM : grad_at + (at + 1) * VDIM]
            keys = keys_ref[head, window, :]
            values = values_ref[window, head * VDIM : (head + 1) * VDIM]
            scores = dot(query, keys, BY_COLUMNS) * SCALE_LOG2 + bias
            expo = jnp.exp2(scores - jnp.max(scores, axis=1, keepdims=True))
            probs = expo * (1.0 / jnp.sum(expo, axis=1, keepdims=True))
            grad_probs = dot(grad, values, BY_COLUMNS)
            delta = jnp.sum(probs * grad_probs, axis=1, keepdims=True)
            grad_scores = (probs * (grad_probs - delta) * SCALE).astype(jnp.bfloat16)
            outs.append(dot(grad_scores, keys, BY_ROWS).astype(jnp.bfloat16))
        dq_ref[rows, :] = jnp.concatenate(outs, axis=1)


def key_kernel(devices, half, here, begun, resident, low_ref, order_ref, source_ref, *refs):
    x_refs = refs[:devices]
    low_rows_ref, keys_ref, values_ref, wk_ref, wv_ref = refs[devices : devices + 5]
    dk_ref, dv_ref, dlat_ref = refs[devices + 5 + begun : devices + 8 + begun]
    x_all, sum_nope, sum_value, sum_rope, sem = refs[devices + 8 + begun :]
    blocks = 2 * devices
    total = blocks * half
    grad_at = here * WIDTH
    copies = []
    for number in range(devices):
        for side in range(2):
            block = order_ref[2 * source_ref[number] + side]
            rows = pl.ds(pl.multiple_of(block * half, 16), half)
            from_rows = pl.ds(side * half, half)
            if resident:
                x_all[rows, :] = x_refs[number][from_rows, :]
                continue
            copy = pltpu.make_async_copy(
                x_refs[number].at[from_rows, :], x_all.at[rows, :], sem.at[2 * number + side]
            )
            copy.start()
            copies.append(copy)
    sum_nope[...] = jnp.zeros_like(sum_nope)
    sum_value[...] = jnp.zeros_like(sum_value)
    sum_rope[...] = jnp.zeros_like(sum_rope)
    for copy in copies:
        copy.wait()

    def tile(first, start, span):
        window = pl.ds(start, span)
        rows = pl.ds(first, TILE)
        key_pos = start + lax.broadcasted_iota(jnp.int32, (span, TILE), 0)
        query_pos = first + lax.broadcasted_iota(jnp.int32, (span, TILE), 1)
        seen = (key_pos <= query_pos) & (key_pos >= low_rows_ref[:, rows])
        bias = jnp.where(seen, 0.0, NEG_FILL)
        def begin(head):
            lanes = slice(head * NOPE, (head + 1) * NOPE)
            query = x_all[rows, head * WIDTH : (head + 1) * WIDTH]
            grad = x_all[rows, grad_at + head * VDIM : grad_at + (head + 1) * VDIM]
            scores = dot(keys_ref[head, window, :], query, BY_COLUMNS)
            return lanes, query, grad, scores, dot(values_ref[window, lanes], grad, BY_COLUMNS)

        def middle(lanes, query, grad, scores, grad_probs):
            scores = scores * SCALE_LOG2 + bias
            expo = jnp.exp2(scores - jnp.max(scores, axis=0, keepdims=True))
            inverse = 1.0 / jnp.sum(expo, axis=0, keepdims=True)
            delta = jnp.sum(expo * grad_probs, axis=0, keepdims=True) * inverse
            probs = expo * inverse
            grad_scores = (probs * (grad_probs - delta)).astype(jnp.bfloat16)
            return lanes, query, grad, probs.astype(jnp.bfloat16), grad_scores

        def end(lanes, query, grad, probs, grad_scores):
            sum_value[window, lanes] += dot(probs, grad, BY_ROWS)
            key_grad = dot(grad_scores, query, BY_ROWS)
            sum_nope[window, lanes] += key_grad[:, :NOPE]
            return key_grad[:, NOPE:]

        rope = 0.0
        opened = [begin(head) for head in range(here)]
        for head in range(here):
            rope = rope + end(*middle(*opened[head]))
        sum_rope[window, :] += rope

    def step(number, carry):
        first = pl.multiple_of(number * TILE, TILE)
        oldest = low_ref[first // half] * half
        need = (first + TILE - oldest + GRAIN - 1) // GRAIN
        for size in sizes:
            below = sizes[sizes.index(size) - 1] if size != sizes[0] else 0

            @pl.when((need <= size) & (need > below))
            def _(size=size):
                start = jnp.maximum(first + TILE - size * GRAIN, 0)
                tile(first, pl.multiple_of(start, 16), size * GRAIN)

        return carry

    most = -(-(devices * half + TILE) // GRAIN)
    sizes = list(range(TILE // GRAIN, most + 1, max(1, most // 8)))
    if sizes[-1] != most:
        sizes.append(most)
    lax.fori_loop(0, total // TILE, step, 0)
    dk_ref[...] = (sum_nope[...] * SCALE).astype(jnp.bfloat16)
    dv_ref[...] = sum_value[...].astype(jnp.bfloat16)
    own = []
    for side in range(2):
        block = order_ref[2 * source_ref[0] + side]
        own.append(pl.ds(pl.multiple_of(block * half, 16), half))

    def take(ref):
        return jnp.concatenate([ref[rows, :] for rows in own], axis=0)

    out = dot(take(dk_ref), wk_ref[...], BY_COLUMNS) + dot(take(dv_ref), wv_ref[...], BY_COLUMNS)
    out = jnp.concatenate([out, take(sum_rope) * SCALE], axis=1)
    if begun:
        out = out + refs[devices + 5][...]
    dlat_ref[...] = out.astype(dlat_ref.dtype)


def swap(array, axis, mask):
    size = lax.axis_size(axis)
    return lax.ppermute(array, axis, [(i, i ^ mask) for i in range(size)])


def gather(own, devices):
    far = [own] + [swap(own, "seq", m) for m in range(2, devices, 2)]
    return far + [swap(x, "seq", 1) for x in far]


def join(array, axis, mask):
    return jnp.concatenate([array, swap(array, axis, mask)], axis=0)


def gather_latent(mine, devices):
    step = devices // 2
    while step:
        mine = join(mine, "seq", step)
        step //= 2
    return mine


def gather_by_line(own, mine, me):
    def along(array, pairs):
        return lax.ppermute(
            array, "seq", [(2 * a + y, 2 * b + y) for a, b in pairs for y in range(2)]
        )

    hold = lax.optimization_barrier
    middle = [(1, 2), (2, 1)]
    outward = [(1, 0), (2, 3)]
    place = me // 2
    inner = (place == 1) | (place == 2)
    piece = mine.shape[0]
    mine = jnp.concatenate([mine] + [swap(mine, "seq", mask) for mask in (4, 2, 6)], axis=0)
    held_own, mine = hold((own, mine))
    near = swap(held_own, "seq", 2)
    third = along(held_own, middle)
    y_own = swap(own, "seq", 1)
    mine = join(mine, "seq", 1)
    near, third, y_own, mine = hold((near, third, y_own, mine))
    fourth = along(near, middle)
    handed = along(third, outward)
    y_near = swap(near, "seq", 1)
    theirs = swap(mine, "head", 2)
    fourth, handed, y_near, mine, theirs = hold((fourth, handed, y_near, mine, theirs))
    third = jnp.where(inner, third, handed)
    last = along(fourth, outward)
    y_third = swap(third, "seq", 1)
    first = lax.axis_index("head") < 2
    mine, theirs = (x.reshape(8, piece, mine.shape[1]) for x in (mine, theirs))
    mine = jnp.concatenate(
        [jnp.where(first, mine, theirs), jnp.where(first, theirs, mine)], axis=1
    ).reshape(16 * piece, mine.shape[2])
    other = swap(mine, "head", 1)
    last, y_third = hold((last, y_third))
    fourth = jnp.where(inner, fourth, last)
    y_fourth = swap(fourth, "seq", 1)
    left = place < 2
    places = [place, place ^ 1, jnp.where(left, 2, 1), jnp.where(left, 3, 0)]
    y = me % 2
    sources = [2 * p + y for p in places] + [2 * p + 1 - y for p in places]
    return [own, near, third, fourth, y_own, y_near, y_third, y_fourth], jnp.stack(sources), mine, other


def shards(queries, latent_rope, w_uk, w_uv, d_out, block_order, block_doc):
    local_rows = queries.shape[0]
    heads = w_uk.shape[1] // NOPE
    devices = lax.axis_size("seq")
    half = local_rows // 2
    total = local_rows * devices
    me = lax.axis_index("seq")
    low = jnp.sum((block_doc[None, :] < block_doc[:, None]).astype(jnp.int32), axis=1)
    low_rows = jnp.repeat(low * half, half).reshape(1, total)

    small = total <= 8 * TILE
    pair = heads if small else 2
    packed = [
        jnp.concatenate(
            [
                queries[:, first * WIDTH : (first + pair) * WIDTH],
                d_out[:, first * VDIM : (first + pair) * VDIM],
            ],
            axis=1,
        )
        for first in range(0, heads, pair)
    ]
    core = lax.axis_index("head") % 2
    where = jnp.stack([me, core]).astype(jnp.int32)
    latent = jnp.pad(latent_rope, ((0, 0), (0, LAT_LANES - D_LAT - ROPE)))
    mine = lax.dynamic_slice_in_dim(latent, core * half, half, axis=0)
    by_line = small and devices == 8 and lax.axis_size("head") == 4
    if by_line:
        mine = lax.dynamic_slice_in_dim(
            mine, lax.axis_index("head") // 2 * (half // 2), half // 2, axis=0
        )
        pieces, sources, mine, other = gather_by_line(packed[0], mine, me)
        gathered = [pieces]
    else:
        mine = gather_latent(mine, devices)
        gathered = [gather(x, devices) for x in packed]
        order = list(range(0, devices, 2)) + list(range(1, devices, 2))
        sources = jnp.stack([me ^ m for m in order])
        other = swap(mine, "head", 1)

    bf16 = jnp.bfloat16
    mebi = 1024 * 1024

    def params(size):
        return pltpu.CompilerParams(vmem_limit_bytes=(size if small else 60) * mebi)

    keys, values, turned, d_queries = pl.pallas_call(
        functools.partial(project_kernel, devices, half, heads, pair, small),
        out_shape=(
            jax.ShapeDtypeStruct((heads, total, WIDTH), bf16),
            jax.ShapeDtypeStruct((total, heads * VDIM), bf16),
            jax.ShapeDtypeStruct((D_LAT, total), bf16),
            jax.ShapeDtypeStruct((local_rows, heads * WIDTH), bf16),
        ),
        in_specs=[SMEM, SMEM, SMEM] + [VMEM if small else HBM] * 2 + [HBM, HBM] + [VMEM] * len(packed),
        out_specs=(VMEM, VMEM, VMEM, VMEM),
        scratch_shapes=[
            pltpu.VMEM((total, LAT_LANES), bf16),
            pltpu.VMEM(w_uk.shape, bf16),
            pltpu.VMEM(w_uv.shape, bf16),
            pltpu.SemaphoreType.DMA((2 * devices,)),
            pltpu.SemaphoreType.DMA((2,)),
        ],
        compiler_params=params(20),
        cost_estimate=pl.CostEstimate(
            flops=20 * 2**30, bytes_accessed=16 * mebi, transcendentals=0
        ),
        name="project",
    )(block_order, low, where, mine, other, w_uk, w_uv, *packed)

    dks, dvs = [], []
    shares = []
    for first in range(0, heads, pair):
        lanes = slice(first * NOPE, (first + pair) * NOPE)
        pieces = gathered[first // pair]
        last = first + pair == heads
        dk, dv, *shares = pl.pallas_call(
            functools.partial(key_kernel, devices, half, pair, len(shares), small),
            out_shape=(
                jax.ShapeDtypeStruct((total, pair * NOPE), bf16),
                jax.ShapeDtypeStruct((total, pair * VDIM), bf16),
                jax.ShapeDtypeStruct((local_rows, D_LAT + ROPE), bf16 if last else jnp.float32),
            ),
            in_specs=[SMEM, SMEM, SMEM] + [VMEM if small else HBM] * devices + [VMEM] * (5 + len(shares)),
            out_specs=(VMEM, VMEM, VMEM),
            scratch_shapes=[
                pltpu.VMEM((total, pair * (WIDTH + VDIM)), bf16),
                pltpu.VMEM((total, pair * NOPE), jnp.float32),
                pltpu.VMEM((total, pair * VDIM), jnp.float32),
                pltpu.VMEM((total, ROPE), jnp.float32),
                pltpu.SemaphoreType.DMA((2 * devices,)),
            ],
            compiler_params=params(28),
            cost_estimate=pl.CostEstimate(
                flops=20 * 2**30, bytes_accessed=16 * mebi, transcendentals=0
            ),
            name="keys",
        )(
            low, block_order, sources, *pieces, low_rows,
            keys[first : first + pair], values[:, lanes], w_uk[:, lanes], w_uv[:, lanes], *shares,
        )
        dks.append(dk)
        dvs.append(dv)
    dk = jnp.concatenate(dks, axis=1)
    dv = jnp.concatenate(dvs, axis=1)
    sent = shares[0]
    dlat = sent.astype(jnp.float32) + swap(sent, "head", 1).astype(jnp.float32)
    dlat, dk, dv = lax.optimization_barrier((dlat, dk, dv))
    step = 2
    while step < lax.axis_size("head"):
        sent = dlat.astype(bf16)
        dlat = sent.astype(jnp.float32) + swap(sent, "head", step).astype(jnp.float32)
        step *= 2
    return (d_queries, dlat, dot(turned, dk, BY_ROWS), dot(turned, dv, BY_ROWS))


def solution(mesh):
    return jax.shard_map(
        shards,
        mesh=mesh,
        in_specs=(
            P("seq", "head"),
            P("seq", None),
            P(None, "head"),
            P(None, "head"),
            P("seq", "head"),
            P(),
            P(),
        ),
        out_specs=(P("seq", "head"), P("seq", None), P(None, "head"), P(None, "head")),
        check_vma=False,
    )
```

```python
import functools
import math

import jax
import jax.numpy as jnp
from jax import lax
from jax.experimental import pallas as pl
from jax.experimental.pallas import tpu as pltpu
from jax.sharding import PartitionSpec as P

D_LAT = 512
ROPE = 64
NOPE = 128
VDIM = 128
WIDTH = NOPE + ROPE
SCALE = WIDTH ** (-0.5)
SCALE_LOG2 = SCALE * math.log2(math.e)
NEG_FILL = -1e30
TILE = 256
GRAIN = 128
LAT_LANES = 640
BY_COLUMNS = (((1,), (1,)), ((), ()))
BY_ROWS = (((1,), (0,)), ((), ()))
SMEM = pl.BlockSpec(memory_space=pltpu.SMEM)
VMEM = pl.BlockSpec(memory_space=pltpu.VMEM)
HBM = pl.BlockSpec(memory_space=pl.ANY)


def dot(a, b, dims):
    return lax.dot_general(a, b, dims, preferred_element_type=jnp.float32)


def project_kernel(
    devices, half, heads, pair, resident, order_ref, low_ref, where_ref, mine_ref, other_ref, wk_in, wv_in, *refs
):
    x_refs = refs[: heads // pair]
    keys_ref, values_ref, turned_ref, dq_ref, latent, wk_ref, wv_ref, sem, weight_sem = refs[heads // pair :]
    blocks = 2 * devices
    total = blocks * half
    me, core = where_ref[0], where_ref[1]
    copies = [
        pltpu.make_async_copy(wk_in, wk_ref, weight_sem.at[0]),
        pltpu.make_async_copy(wv_in, wv_ref, weight_sem.at[1]),
    ]
    for copy in copies:
        copy.start()
    masks = [0]
    for bit in reversed(range(devices.bit_length() - 1)):
        masks = masks + [m ^ (1 << bit) for m in masks]
    for number, mask in enumerate(masks):
        for side, source in enumerate((mine_ref, other_ref)):
            block = order_ref[2 * (me ^ mask) + (core ^ side)]
            rows = pl.ds(pl.multiple_of(block * half, 16), half)
            from_rows = pl.ds(number * half, half)
            if resident:
                latent[rows, :] = source[from_rows, :]
                continue
            copy = pltpu.make_async_copy(
                source.at[from_rows, :], latent.at[rows, :], sem.at[2 * number + side]
            )
            copy.start()
            copies.append(copy)
    for copy in copies:
        copy.wait()
    for first in range(0, total, TILE):
        rows = pl.ds(first, TILE)
        part = latent[rows, :D_LAT]
        rope = latent[rows, D_LAT : D_LAT + ROPE]
        up_keys = dot(part, wk_ref[...], BY_ROWS).astype(jnp.bfloat16)
        for head in range(heads):
            keys_ref[head, rows, :] = jnp.concatenate(
                [up_keys[:, head * NOPE : (head + 1) * NOPE], rope], axis=1
            )
        values_ref[rows, :] = dot(part, wv_ref[...], BY_ROWS).astype(jnp.bfloat16)
        turned_ref[:, first : first + TILE] = part.T
    span = (blocks // 2) * half
    grad_at = pair * WIDTH
    for side in range(2):
        block = order_ref[2 * me + side]
        start = pl.multiple_of(jnp.maximum(block - (blocks // 2 - 1), 0) * half, 16)
        window = pl.ds(start, span)
        key_pos = start + lax.broadcasted_iota(jnp.int32, (half, span), 1)
        query_pos = block * half + lax.broadcasted_iota(jnp.int32, (half, span), 0)
        seen = (key_pos <= query_pos) & (key_pos >= low_ref[block] * half)
        bias = jnp.where(seen, 0.0, NEG_FILL)
        rows = pl.ds(side * half, half)
        opened = []
        for head in range(heads):
            x_ref, at = x_refs[head // pair], head % pair
            query = x_ref[rows, at * WIDTH : (at + 1) * WIDTH]
            grad = x_ref[rows, grad_at + at * VDIM : grad_at + (at + 1) * VDIM]
            values = values_ref[window, head * VDIM : (head + 1) * VDIM]
            scores = dot(query, keys_ref[head, window, :], BY_COLUMNS)
            opened.append((scores, dot(grad, values, BY_COLUMNS)))
        outs = []
        for head, (scores, grad_probs) in enumerate(opened):
            scores = scores * SCALE_LOG2 + bias
            expo = jnp.exp2(scores - jnp.max(scores, axis=1, keepdims=True))
            probs = expo * (1.0 / jnp.sum(expo, axis=1, keepdims=True))
            delta = jnp.sum(probs * grad_probs, axis=1, keepdims=True)
            grad_scores = (probs * (grad_probs - delta) * SCALE).astype(jnp.bfloat16)
            keys = keys_ref[head, window, :]
            outs.append(dot(grad_scores, keys, BY_ROWS).astype(jnp.bfloat16))
        dq_ref[rows, :] = jnp.concatenate(outs, axis=1)


def key_kernel(devices, half, here, begun, resident, low_ref, order_ref, source_ref, *refs):
    x_refs = refs[:devices]
    low_rows_ref, keys_ref, values_ref, wk_ref, wv_ref = refs[devices : devices + 5]
    dk_ref, dv_ref, dlat_ref = refs[devices + 5 + begun : devices + 8 + begun]
    x_all, sum_nope, sum_value, sum_rope, sem = refs[devices + 8 + begun :]
    blocks = 2 * devices
    total = blocks * half
    grad_at = here * WIDTH
    copies = []
    for number in range(devices):
        for side in range(2):
            block = order_ref[2 * source_ref[number] + side]
            rows = pl.ds(pl.multiple_of(block * half, 16), half)
            from_rows = pl.ds(side * half, half)
            if resident:
                x_all[rows, :] = x_refs[number][from_rows, :]
                continue
            copy = pltpu.make_async_copy(
                x_refs[number].at[from_rows, :], x_all.at[rows, :], sem.at[2 * number + side]
            )
            copy.start()
            copies.append(copy)
    sum_nope[...] = jnp.zeros_like(sum_nope)
    sum_value[...] = jnp.zeros_like(sum_value)
    sum_rope[...] = jnp.zeros_like(sum_rope)
    for copy in copies:
        copy.wait()

    def tile(first, start, span):
        window = pl.ds(start, span)
        rows = pl.ds(first, TILE)
        key_pos = start + lax.broadcasted_iota(jnp.int32, (span, TILE), 0)
        query_pos = first + lax.broadcasted_iota(jnp.int32, (span, TILE), 1)
        seen = (key_pos <= query_pos) & (key_pos >= low_rows_ref[:, rows])
        bias = jnp.where(seen, 0.0, NEG_FILL)
        def begin(head):
            lanes = slice(head * NOPE, (head + 1) * NOPE)
            query = x_all[rows, head * WIDTH : (head + 1) * WIDTH]
            grad = x_all[rows, grad_at + head * VDIM : grad_at + (head + 1) * VDIM]
            scores = dot(keys_ref[head, window, :], query, BY_COLUMNS)
            return lanes, query, grad, scores, dot(values_ref[window, lanes], grad, BY_COLUMNS)

        def middle(lanes, query, grad, scores, grad_probs):
            scores = scores * SCALE_LOG2 + bias
            expo = jnp.exp2(scores - jnp.max(scores, axis=0, keepdims=True))
            inverse = 1.0 / jnp.sum(expo, axis=0, keepdims=True)
            delta = jnp.sum(expo * grad_probs, axis=0, keepdims=True) * inverse
            probs = expo * inverse
            grad_scores = (probs * (grad_probs - delta)).astype(jnp.bfloat16)
            return lanes, query, grad, probs.astype(jnp.bfloat16), grad_scores

        def end(lanes, query, grad, probs, grad_scores):
            sum_value[window, lanes] += dot(probs, grad, BY_ROWS)
            key_grad = dot(grad_scores, query, BY_ROWS)
            sum_nope[window, lanes] += key_grad[:, :NOPE]
            return key_grad[:, NOPE:]

        rope = 0.0
        opened = [begin(head) for head in range(here)]
        for head in range(here):
            rope = rope + end(*middle(*opened[head]))
        sum_rope[window, :] += rope

    def step(number, carry):
        first = pl.multiple_of(number * TILE, TILE)
        oldest = low_ref[first // half] * half
        need = (first + TILE - oldest + GRAIN - 1) // GRAIN
        for size in sizes:
            below = sizes[sizes.index(size) - 1] if size != sizes[0] else 0

            @pl.when((need <= size) & (need > below))
            def _(size=size):
                start = jnp.maximum(first + TILE - size * GRAIN, 0)
                tile(first, pl.multiple_of(start, 16), size * GRAIN)

        return carry

    most = -(-(devices * half + TILE) // GRAIN)
    sizes = list(range(TILE // GRAIN, most + 1, max(1, most // 8)))
    if sizes[-1] != most:
        sizes.append(most)
    lax.fori_loop(0, total // TILE, step, 0)
    dk_ref[...] = (sum_nope[...] * SCALE).astype(jnp.bfloat16)
    dv_ref[...] = sum_value[...].astype(jnp.bfloat16)
    own = []
    for side in range(2):
        block = order_ref[2 * source_ref[0] + side]
        own.append(pl.ds(pl.multiple_of(block * half, 16), half))

    def take(ref):
        return jnp.concatenate([ref[rows, :] for rows in own], axis=0)

    out = dot(take(dk_ref), wk_ref[...], BY_COLUMNS) + dot(take(dv_ref), wv_ref[...], BY_COLUMNS)
    out = jnp.concatenate([out, take(sum_rope) * SCALE], axis=1)
    if begun:
        out = out + refs[devices + 5][...]
    dlat_ref[...] = out.astype(dlat_ref.dtype)


def swap(array, axis, mask):
    size = lax.axis_size(axis)
    return lax.ppermute(array, axis, [(i, i ^ mask) for i in range(size)])


def gather(own, devices):
    far = [own] + [swap(own, "seq", m) for m in range(2, devices, 2)]
    return far + [swap(x, "seq", 1) for x in far]


def join(array, axis, mask):
    return jnp.concatenate([array, swap(array, axis, mask)], axis=0)


def gather_latent(mine, devices):
    step = devices // 2
    while step:
        mine = join(mine, "seq", step)
        step //= 2
    return mine


def gather_by_line(own, mine, me):
    def along(array, pairs):
        return lax.ppermute(
            array, "seq", [(2 * a + y, 2 * b + y) for a, b in pairs for y in range(2)]
        )

    hold = lax.optimization_barrier
    middle = [(1, 2), (2, 1)]
    outward = [(1, 0), (2, 3)]
    place = me // 2
    inner = (place == 1) | (place == 2)
    piece = mine.shape[0]
    mine = jnp.concatenate([mine] + [swap(mine, "seq", mask) for mask in (4, 2, 6)], axis=0)
    held_own, mine = hold((own, mine))
    near = swap(held_own, "seq", 2)
    third = along(held_own, middle)
    y_own = swap(own, "seq", 1)
    mine = join(mine, "seq", 1)
    near, third, y_own, mine = hold((near, third, y_own, mine))
    fourth = along(near, middle)
    handed = along(third, outward)
    y_near = swap(near, "seq", 1)
    theirs = swap(mine, "head", 2)
    fourth, handed, y_near, mine, theirs = hold((fourth, handed, y_near, mine, theirs))
    third = jnp.where(inner, third, handed)
    last = along(fourth, outward)
    y_third = swap(third, "seq", 1)
    first = lax.axis_index("head") < 2
    mine, theirs = (x.reshape(8, piece, mine.shape[1]) for x in (mine, theirs))
    mine = jnp.concatenate(
        [jnp.where(first, mine, theirs), jnp.where(first, theirs, mine)], axis=1
    ).reshape(16 * piece, mine.shape[2])
    other = swap(mine, "head", 1)
    last, y_third = hold((last, y_third))
    fourth = jnp.where(inner, fourth, last)
    y_fourth = swap(fourth, "seq", 1)
    left = place < 2
    places = [place, place ^ 1, jnp.where(left, 2, 1), jnp.where(left, 3, 0)]
    y = me % 2
    sources = [2 * p + y for p in places] + [2 * p + 1 - y for p in places]
    return [own, near, third, fourth, y_own, y_near, y_third, y_fourth], jnp.stack(sources), mine, other


def shards(queries, latent_rope, w_uk, w_uv, d_out, block_order, block_doc):
    local_rows = queries.shape[0]
    heads = w_uk.shape[1] // NOPE
    devices = lax.axis_size("seq")
    half = local_rows // 2
    total = local_rows * devices
    me = lax.axis_index("seq")
    low = jnp.sum((block_doc[None, :] < block_doc[:, None]).astype(jnp.int32), axis=1)
    low_rows = jnp.repeat(low * half, half).reshape(1, total)

    small = total <= 8 * TILE
    pair = heads if small else 2
    packed = [
        jnp.concatenate(
            [
                queries[:, first * WIDTH : (first + pair) * WIDTH],
                d_out[:, first * VDIM : (first + pair) * VDIM],
            ],
            axis=1,
        )
        for first in range(0, heads, pair)
    ]
    core = lax.axis_index("head") % 2
    where = jnp.stack([me, core]).astype(jnp.int32)
    latent = jnp.pad(latent_rope, ((0, 0), (0, LAT_LANES - D_LAT - ROPE)))
    mine = lax.dynamic_slice_in_dim(latent, core * half, half, axis=0)
    by_line = small and devices == 8 and lax.axis_size("head") == 4
    if by_line:
        mine = lax.dynamic_slice_in_dim(
            mine, lax.axis_index("head") // 2 * (half // 2), half // 2, axis=0
        )
        pieces, sources, mine, other = gather_by_line(packed[0], mine, me)
        gathered = [pieces]
    else:
        mine = gather_latent(mine, devices)
        gathered = [gather(x, devices) for x in packed]
        order = list(range(0, devices, 2)) + list(range(1, devices, 2))
        sources = jnp.stack([me ^ m for m in order])
        other = swap(mine, "head", 1)

    bf16 = jnp.bfloat16
    mebi = 1024 * 1024

    def params(size):
        return pltpu.CompilerParams(vmem_limit_bytes=(size if small else 60) * mebi)

    keys, values, turned, d_queries = pl.pallas_call(
        functools.partial(project_kernel, devices, half, heads, pair, small),
        out_shape=(
            jax.ShapeDtypeStruct((heads, total, WIDTH), bf16),
            jax.ShapeDtypeStruct((total, heads * VDIM), bf16),
            jax.ShapeDtypeStruct((D_LAT, total), bf16),
            jax.ShapeDtypeStruct((local_rows, heads * WIDTH), bf16),
        ),
        in_specs=[SMEM, SMEM, SMEM] + [VMEM if small else HBM] * 2 + [HBM, HBM] + [VMEM] * len(packed),
        out_specs=(VMEM, VMEM, VMEM, VMEM),
        scratch_shapes=[
            pltpu.VMEM((total, LAT_LANES), bf16),
            pltpu.VMEM(w_uk.shape, bf16),
            pltpu.VMEM(w_uv.shape, bf16),
            pltpu.SemaphoreType.DMA((2 * devices,)),
            pltpu.SemaphoreType.DMA((2,)),
        ],
        compiler_params=params(20),
        cost_estimate=pl.CostEstimate(
            flops=20 * 2**30, bytes_accessed=16 * mebi, transcendentals=0
        ),
        name="project",
    )(block_order, low, where, mine, other, w_uk, w_uv, *packed)

    dks, dvs = [], []
    shares = []
    for first in range(0, heads, pair):
        lanes = slice(first * NOPE, (first + pair) * NOPE)
        pieces = gathered[first // pair]
        last = first + pair == heads
        dk, dv, *shares = pl.pallas_call(
            functools.partial(key_kernel, devices, half, pair, len(shares), small),
            out_shape=(
                jax.ShapeDtypeStruct((total, pair * NOPE), bf16),
                jax.ShapeDtypeStruct((total, pair * VDIM), bf16),
                jax.ShapeDtypeStruct((local_rows, D_LAT + ROPE), bf16 if last else jnp.float32),
            ),
            in_specs=[SMEM, SMEM, SMEM] + [VMEM if small else HBM] * devices + [VMEM] * (5 + len(shares)),
            out_specs=(VMEM, VMEM, VMEM),
            scratch_shapes=[
                pltpu.VMEM((total, pair * (WIDTH + VDIM)), bf16),
                pltpu.VMEM((total, pair * NOPE), jnp.float32),
                pltpu.VMEM((total, pair * VDIM), jnp.float32),
                pltpu.VMEM((total, ROPE), jnp.float32),
                pltpu.SemaphoreType.DMA((2 * devices,)),
            ],
            compiler_params=params(28),
            cost_estimate=pl.CostEstimate(
                flops=20 * 2**30, bytes_accessed=16 * mebi, transcendentals=0
            ),
            name="keys",
        )(
            low, block_order, sources, *pieces, low_rows,
            keys[first : first + pair], values[:, lanes], w_uk[:, lanes], w_uv[:, lanes], *shares,
        )
        dks.append(dk)
        dvs.append(dv)
    dk = jnp.concatenate(dks, axis=1)
    dv = jnp.concatenate(dvs, axis=1)
    sent = shares[0]
    dlat = sent.astype(jnp.float32) + swap(sent, "head", 1).astype(jnp.float32)
    dlat, dk, dv = lax.optimization_barrier((dlat, dk, dv))
    step = 2
    while step < lax.axis_size("head"):
        sent = dlat.astype(bf16)
        dlat = sent.astype(jnp.float32) + swap(sent, "head", step).astype(jnp.float32)
        step *= 2
    return (d_queries, dlat, dot(turned, dk, BY_ROWS), dot(turned, dv, BY_ROWS))


def solution(mesh):
    return jax.shard_map(
        shards,
        mesh=mesh,
        in_specs=(
            P("seq", "head"),
            P("seq", None),
            P(None, "head"),
            P(None, "head"),
            P("seq", "head"),
            P(),
            P(),
        ),
        out_specs=(P("seq", "head"), P("seq", None), P(None, "head"), P(None, "head")),
        check_vma=False,
    )
```

```python
import functools
import math

import jax
import jax.numpy as jnp
from jax import lax
from jax.experimental import pallas as pl
from jax.experimental.pallas import tpu as pltpu
from jax.sharding import PartitionSpec as P

D_LAT = 512
ROPE = 64
NOPE = 128
VDIM = 128
WIDTH = NOPE + ROPE
SCALE = WIDTH ** (-0.5)
SCALE_LOG2 = SCALE * math.log2(math.e)
NEG_FILL = -1e30
TILE = 256
GRAIN = 128
LAT_LANES = 640
BY_COLUMNS = (((1,), (1,)), ((), ()))
BY_ROWS = (((1,), (0,)), ((), ()))
SMEM = pl.BlockSpec(memory_space=pltpu.SMEM)
VMEM = pl.BlockSpec(memory_space=pltpu.VMEM)
HBM = pl.BlockSpec(memory_space=pl.ANY)


def dot(a, b, dims):
    return lax.dot_general(a, b, dims, preferred_element_type=jnp.float32)


def project_kernel(
    devices, half, heads, pair, resident, order_ref, low_ref, where_ref, mine_ref, other_ref, wk_in, wv_in, *refs
):
    x_refs = refs[: heads // pair]
    keys_ref, values_ref, turned_ref, dq_ref, latent, wk_ref, wv_ref, sem, weight_sem = refs[heads // pair :]
    blocks = 2 * devices
    total = blocks * half
    me, core = where_ref[0], where_ref[1]
    copies = [
        pltpu.make_async_copy(wk_in, wk_ref, weight_sem.at[0]),
        pltpu.make_async_copy(wv_in, wv_ref, weight_sem.at[1]),
    ]
    for copy in copies:
        copy.start()
    masks = [0]
    for bit in reversed(range(devices.bit_length() - 1)):
        masks = masks + [m ^ (1 << bit) for m in masks]
    for number, mask in enumerate(masks):
        for side, source in enumerate((mine_ref, other_ref)):
            block = order_ref[2 * (me ^ mask) + (core ^ side)]
            rows = pl.ds(pl.multiple_of(block * half, 16), half)
            from_rows = pl.ds(number * half, half)
            if resident:
                latent[rows, :] = source[from_rows, :]
                continue
            copy = pltpu.make_async_copy(
                source.at[from_rows, :], latent.at[rows, :], sem.at[2 * number + side]
            )
            copy.start()
            copies.append(copy)
    for copy in copies:
        copy.wait()
    for first in range(0, total, TILE):
        rows = pl.ds(first, TILE)
        part = latent[rows, :D_LAT]
        rope = latent[rows, D_LAT : D_LAT + ROPE]
        up_keys = dot(part, wk_ref[...], BY_ROWS).astype(jnp.bfloat16)
        for head in range(heads):
            keys_ref[head, rows, :] = jnp.concatenate(
                [up_keys[:, head * NOPE : (head + 1) * NOPE], rope], axis=1
            )
        values_ref[rows, :] = dot(part, wv_ref[...], BY_ROWS).astype(jnp.bfloat16)
        turned_ref[:, first : first + TILE] = part.T
    span = (blocks // 2) * half
    grad_at = pair * WIDTH
    for side in range(2):
        block = order_ref[2 * me + side]
        start = pl.multiple_of(jnp.maximum(block - (blocks // 2 - 1), 0) * half, 16)
        window = pl.ds(start, span)
        key_pos = start + lax.broadcasted_iota(jnp.int32, (half, span), 1)
        query_pos = block * half + lax.broadcasted_iota(jnp.int32, (half, span), 0)
        seen = (key_pos <= query_pos) & (key_pos >= low_ref[block] * half)
        bias = jnp.where(seen, 0.0, NEG_FILL)
        rows = pl.ds(side * half, half)
        opened = []
        for head in range(heads):
            x_ref, at = x_refs[head // pair], head % pair
            query = x_ref[rows, at * WIDTH : (at + 1) * WIDTH]
            grad = x_ref[rows, grad_at + at * VDIM : grad_at + (at + 1) * VDIM]
            values = values_ref[window, head * VDIM : (head + 1) * VDIM]
            scores = dot(query, keys_ref[head, window, :], BY_COLUMNS)
            opened.append((scores, dot(grad, values, BY_COLUMNS)))
        outs = []
        for head, (scores, grad_probs) in enumerate(opened):
            scores = scores * SCALE_LOG2 + bias
            expo = jnp.exp2(scores - jnp.max(scores, axis=1, keepdims=True))
            probs = expo * (1.0 / jnp.sum(expo, axis=1, keepdims=True))
            delta = jnp.sum(probs * grad_probs, axis=1, keepdims=True)
            grad_scores = (probs * (grad_probs - delta) * SCALE).astype(jnp.bfloat16)
            keys = keys_ref[head, window, :]
            outs.append(dot(grad_scores, keys, BY_ROWS).astype(jnp.bfloat16))
        dq_ref[rows, :] = jnp.concatenate(outs, axis=1)


def key_kernel(devices, half, here, begun, resident, low_ref, order_ref, source_ref, *refs):
    x_refs = refs[:devices]
    low_rows_ref, keys_ref, values_ref, wk_ref, wv_ref = refs[devices : devices + 5]
    dk_ref, dv_ref, dlat_ref = refs[devices + 5 + begun : devices + 8 + begun]
    x_all, sum_nope, sum_value, sum_rope, sem = refs[devices + 8 + begun :]
    blocks = 2 * devices
    total = blocks * half
    grad_at = here * WIDTH
    copies = []
    for number in range(devices):
        for side in range(2):
            block = order_ref[2 * source_ref[number] + side]
            rows = pl.ds(pl.multiple_of(block * half, 16), half)
            from_rows = pl.ds(side * half, half)
            if resident:
                x_all[rows, :] = x_refs[number][from_rows, :]
                continue
            copy = pltpu.make_async_copy(
                x_refs[number].at[from_rows, :], x_all.at[rows, :], sem.at[2 * number + side]
            )
            copy.start()
            copies.append(copy)
    sum_nope[...] = jnp.zeros_like(sum_nope)
    sum_value[...] = jnp.zeros_like(sum_value)
    sum_rope[...] = jnp.zeros_like(sum_rope)
    for copy in copies:
        copy.wait()

    def tile(first, start, span):
        window = pl.ds(start, span)
        rows = pl.ds(first, TILE)
        key_pos = start + lax.broadcasted_iota(jnp.int32, (span, TILE), 0)
        query_pos = first + lax.broadcasted_iota(jnp.int32, (span, TILE), 1)
        seen = (key_pos <= query_pos) & (key_pos >= low_rows_ref[:, rows])
        bias = jnp.where(seen, 0.0, NEG_FILL)
        def begin(head):
            lanes = slice(head * NOPE, (head + 1) * NOPE)
            query = x_all[rows, head * WIDTH : (head + 1) * WIDTH]
            grad = x_all[rows, grad_at + head * VDIM : grad_at + (head + 1) * VDIM]
            scores = dot(keys_ref[head, window, :], query, BY_COLUMNS)
            return lanes, query, grad, scores, dot(values_ref[window, lanes], grad, BY_COLUMNS)

        def middle(lanes, query, grad, scores, grad_probs):
            scores = scores * SCALE_LOG2 + bias
            expo = jnp.exp2(scores - jnp.max(scores, axis=0, keepdims=True))
            inverse = 1.0 / jnp.sum(expo, axis=0, keepdims=True)
            delta = jnp.sum(expo * grad_probs, axis=0, keepdims=True) * inverse
            probs = expo * inverse
            grad_scores = (probs * (grad_probs - delta)).astype(jnp.bfloat16)
            return lanes, query, grad, probs.astype(jnp.bfloat16), grad_scores

        def end(lanes, query, grad, probs, grad_scores):
            sum_value[window, lanes] += dot(probs, grad, BY_ROWS)
            key_grad = dot(grad_scores, query, BY_ROWS)
            sum_nope[window, lanes] += key_grad[:, :NOPE]
            return key_grad[:, NOPE:]

        rope = 0.0
        weighed = None
        for opened in [begin(head) for head in range(here)]:
            following = middle(*opened)
            if weighed is not None:
                rope = rope + end(*weighed)
            weighed = following
        rope = rope + end(*weighed)
        sum_rope[window, :] += rope

    def step(number, carry):
        first = pl.multiple_of(number * TILE, TILE)
        oldest = low_ref[first // half] * half
        need = (first + TILE - oldest + GRAIN - 1) // GRAIN
        for size in sizes:
            below = sizes[sizes.index(size) - 1] if size != sizes[0] else 0

            @pl.when((need <= size) & (need > below))
            def _(size=size):
                start = jnp.maximum(first + TILE - size * GRAIN, 0)
                tile(first, pl.multiple_of(start, 16), size * GRAIN)

        return carry

    most = -(-(devices * half + TILE) // GRAIN)
    sizes = list(range(TILE // GRAIN, most + 1, max(1, most // 8)))
    if sizes[-1] != most:
        sizes.append(most)
    lax.fori_loop(0, total // TILE, step, 0)
    dk_ref[...] = (sum_nope[...] * SCALE).astype(jnp.bfloat16)
    dv_ref[...] = sum_value[...].astype(jnp.bfloat16)
    own = []
    for side in range(2):
        block = order_ref[2 * source_ref[0] + side]
        own.append(pl.ds(pl.multiple_of(block * half, 16), half))

    def take(ref):
        return jnp.concatenate([ref[rows, :] for rows in own], axis=0)

    out = dot(take(dk_ref), wk_ref[...], BY_COLUMNS) + dot(take(dv_ref), wv_ref[...], BY_COLUMNS)
    out = jnp.concatenate([out, take(sum_rope) * SCALE], axis=1)
    if begun:
        out = out + refs[devices + 5][...]
    dlat_ref[...] = out.astype(dlat_ref.dtype)


def swap(array, axis, mask):
    size = lax.axis_size(axis)
    return lax.ppermute(array, axis, [(i, i ^ mask) for i in range(size)])


def gather(own, devices):
    far = [own] + [swap(own, "seq", m) for m in range(2, devices, 2)]
    return far + [swap(x, "seq", 1) for x in far]


def join(array, axis, mask):
    return jnp.concatenate([array, swap(array, axis, mask)], axis=0)


def gather_latent(mine, devices):
    step = devices // 2
    while step:
        mine = join(mine, "seq", step)
        step //= 2
    return mine


def gather_by_line(own, mine, me):
    def along(array, pairs):
        return lax.ppermute(
            array, "seq", [(2 * a + y, 2 * b + y) for a, b in pairs for y in range(2)]
        )

    hold = lax.optimization_barrier
    middle = [(1, 2), (2, 1)]
    outward = [(1, 0), (2, 3)]
    place = me // 2
    inner = (place == 1) | (place == 2)
    piece = mine.shape[0]
    mine = jnp.concatenate([mine] + [swap(mine, "seq", mask) for mask in (4, 2, 6)], axis=0)
    held_own, mine = hold((own, mine))
    near = swap(held_own, "seq", 2)
    third = along(held_own, middle)
    y_own = swap(own, "seq", 1)
    mine = join(mine, "seq", 1)
    near, third, y_own, mine = hold((near, third, y_own, mine))
    fourth = along(near, middle)
    handed = along(third, outward)
    y_near = swap(near, "seq", 1)
    theirs = swap(mine, "head", 2)
    fourth, handed, y_near, mine, theirs = hold((fourth, handed, y_near, mine, theirs))
    third = jnp.where(inner, third, handed)
    last = along(fourth, outward)
    y_third = swap(third, "seq", 1)
    first = lax.axis_index("head") < 2
    mine, theirs = (x.reshape(8, piece, mine.shape[1]) for x in (mine, theirs))
    mine = jnp.concatenate(
        [jnp.where(first, mine, theirs), jnp.where(first, theirs, mine)], axis=1
    ).reshape(16 * piece, mine.shape[2])
    other = swap(mine, "head", 1)
    last, y_third = hold((last, y_third))
    fourth = jnp.where(inner, fourth, last)
    y_fourth = swap(fourth, "seq", 1)
    left = place < 2
    places = [place, place ^ 1, jnp.where(left, 2, 1), jnp.where(left, 3, 0)]
    y = me % 2
    sources = [2 * p + y for p in places] + [2 * p + 1 - y for p in places]
    return [own, near, third, fourth, y_own, y_near, y_third, y_fourth], jnp.stack(sources), mine, other


def shards(queries, latent_rope, w_uk, w_uv, d_out, block_order, block_doc):
    local_rows = queries.shape[0]
    heads = w_uk.shape[1] // NOPE
    devices = lax.axis_size("seq")
    half = local_rows // 2
    total = local_rows * devices
    me = lax.axis_index("seq")
    low = jnp.sum((block_doc[None, :] < block_doc[:, None]).astype(jnp.int32), axis=1)
    low_rows = jnp.repeat(low * half, half).reshape(1, total)

    small = total <= 8 * TILE
    pair = heads if small else 2
    packed = [
        jnp.concatenate(
            [
                queries[:, first * WIDTH : (first + pair) * WIDTH],
                d_out[:, first * VDIM : (first + pair) * VDIM],
            ],
            axis=1,
        )
        for first in range(0, heads, pair)
    ]
    core = lax.axis_index("head") % 2
    where = jnp.stack([me, core]).astype(jnp.int32)
    latent = jnp.pad(latent_rope, ((0, 0), (0, LAT_LANES - D_LAT - ROPE)))
    mine = lax.dynamic_slice_in_dim(latent, core * half, half, axis=0)
    by_line = small and devices == 8 and lax.axis_size("head") == 4
    if by_line:
        mine = lax.dynamic_slice_in_dim(
            mine, lax.axis_index("head") // 2 * (half // 2), half // 2, axis=0
        )
        pieces, sources, mine, other = gather_by_line(packed[0], mine, me)
        gathered = [pieces]
    else:
        mine = gather_latent(mine, devices)
        gathered = [gather(x, devices) for x in packed]
        order = list(range(0, devices, 2)) + list(range(1, devices, 2))
        sources = jnp.stack([me ^ m for m in order])
        other = swap(mine, "head", 1)

    bf16 = jnp.bfloat16
    mebi = 1024 * 1024

    def params(size):
        return pltpu.CompilerParams(vmem_limit_bytes=(size if small else 60) * mebi)

    keys, values, turned, d_queries = pl.pallas_call(
        functools.partial(project_kernel, devices, half, heads, pair, small),
        out_shape=(
            jax.ShapeDtypeStruct((heads, total, WIDTH), bf16),
            jax.ShapeDtypeStruct((total, heads * VDIM), bf16),
            jax.ShapeDtypeStruct((D_LAT, total), bf16),
            jax.ShapeDtypeStruct((local_rows, heads * WIDTH), bf16),
        ),
        in_specs=[SMEM, SMEM, SMEM] + [VMEM if small else HBM] * 2 + [HBM, HBM] + [VMEM] * len(packed),
        out_specs=(VMEM, VMEM, VMEM, VMEM),
        scratch_shapes=[
            pltpu.VMEM((total, LAT_LANES), bf16),
            pltpu.VMEM(w_uk.shape, bf16),
            pltpu.VMEM(w_uv.shape, bf16),
            pltpu.SemaphoreType.DMA((2 * devices,)),
            pltpu.SemaphoreType.DMA((2,)),
        ],
        compiler_params=params(20),
        cost_estimate=pl.CostEstimate(
            flops=20 * 2**30, bytes_accessed=16 * mebi, transcendentals=0
        ),
        name="project",
    )(block_order, low, where, mine, other, w_uk, w_uv, *packed)

    dks, dvs = [], []
    shares = []
    for first in range(0, heads, pair):
        lanes = slice(first * NOPE, (first + pair) * NOPE)
        pieces = gathered[first // pair]
        last = first + pair == heads
        dk, dv, *shares = pl.pallas_call(
            functools.partial(key_kernel, devices, half, pair, len(shares), small),
            out_shape=(
                jax.ShapeDtypeStruct((total, pair * NOPE), bf16),
                jax.ShapeDtypeStruct((total, pair * VDIM), bf16),
                jax.ShapeDtypeStruct((local_rows, D_LAT + ROPE), bf16 if last else jnp.float32),
            ),
            in_specs=[SMEM, SMEM, SMEM] + [VMEM if small else HBM] * devices + [VMEM] * (5 + len(shares)),
            out_specs=(VMEM, VMEM, VMEM),
            scratch_shapes=[
                pltpu.VMEM((total, pair * (WIDTH + VDIM)), bf16),
                pltpu.VMEM((total, pair * NOPE), jnp.float32),
                pltpu.VMEM((total, pair * VDIM), jnp.float32),
                pltpu.VMEM((total, ROPE), jnp.float32),
                pltpu.SemaphoreType.DMA((2 * devices,)),
            ],
            compiler_params=params(28),
            cost_estimate=pl.CostEstimate(
                flops=20 * 2**30, bytes_accessed=16 * mebi, transcendentals=0
            ),
            name="keys",
        )(
            low, block_order, sources, *pieces, low_rows,
            keys[first : first + pair], values[:, lanes], w_uk[:, lanes], w_uv[:, lanes], *shares,
        )
        dks.append(dk)
        dvs.append(dv)
    dk = jnp.concatenate(dks, axis=1)
    dv = jnp.concatenate(dvs, axis=1)
    sent = shares[0]
    dlat = sent.astype(jnp.float32) + swap(sent, "head", 1).astype(jnp.float32)
    dlat, dk, dv = lax.optimization_barrier((dlat, dk, dv))
    step = 2
    while step < lax.axis_size("head"):
        sent = dlat.astype(bf16)
        dlat = sent.astype(jnp.float32) + swap(sent, "head", step).astype(jnp.float32)
        step *= 2
    return (d_queries, dlat, dot(turned, dk, BY_ROWS), dot(turned, dv, BY_ROWS))


def solution(mesh):
    return jax.shard_map(
        shards,
        mesh=mesh,
        in_specs=(
            P("seq", "head"),
            P("seq", None),
            P(None, "head"),
            P(None, "head"),
            P("seq", "head"),
            P(),
            P(),
        ),
        out_specs=(P("seq", "head"), P("seq", None), P(None, "head"), P(None, "head")),
        check_vma=False,
    )
```
